32 devices in a mesh: row: 4 (over y, core), col: 8 (over z, x).
Axes of the slice: x: 2, y: 2, z: 4, core: 2. Of those that a mesh axis runs over, the one named last changes fastest.
Arguments:
- user_factors: bfloat16 [16384, 64], P(('row', 'col')), may hold values from -4 to 4
- item_factors: bfloat16 [16384, 64], P(('col', 'row')), may hold values from -4 to 4
- start_vectors: bfloat16 [16384, 128], P(('col', 'row')), may hold values from -6 to 6
- ratings: bfloat16 [4, 8, 96, 128, 128], P('row', 'col'), may hold values from -6 to 6
- tile_rows: int32 [4, 8, 96], P('row', 'col'), may hold values from 0 to 31, as said below
- tile_cols: int32 [4, 8, 96], P('row', 'col'), may hold values from 0 to 15, as said below
- tile_count: int32 [4, 8], P('row', 'col'), may hold values from 32 to 96, as said below
Outputs:
- user_basis_out: float32 [16384, 128], P(('row', 'col'))
- item_basis_out: float32 [16384, 128], P(('col', 'row'))
The draws below stay inside these ranges and needn't reach their ends.
Inputs may be any that keep to these rules, and one draw needn't show every extreme that they name: `tile_rows`: within one device the slots name distinct tiles of its blocks. `tile_cols`: within one device the slots name distinct tiles of its blocks. `tile_count`: some device uses all 96 slots in every draw; slots at or past a device's count are unused.
All inputs are finite; a program needn't handle non-finite values.
Results may differ from the reference program's by a relative error of at most 0.009.
Values may be sent and summed in bfloat16 or wider, within the bound.
A program may use at most 64 MiB of HBM per device.

```python
import jax
import jax.numpy as jnp
from jax import lax

TILE = 128
R = 64
VECS = 128
TU = 32
TI = 16
K = 96
USERS = 16384
ITEMS = 16384
N_ROW = 4
N_COL = 8


def tile_pairs(key):
    keys = jax.random.split(key, N_ROW * N_COL)
    picks = jax.vmap(lambda single: jax.random.permutation(single, TU * TI)[:K])(keys)
    return picks.reshape(N_ROW, N_COL, K).astype(jnp.int32)


def draw_tile_rows(key, part):
    picks = tile_pairs(key)
    return (picks // TI).astype(jnp.int32)


def draw_tile_cols(key, part):
    picks = tile_pairs(key)
    return (picks % TI).astype(jnp.int32)


def draw_tile_count(key, part):
    key = jax.random.fold_in(key, 7)
    first, second = jax.random.split(key)
    counts = jax.random.randint(first, (N_ROW * N_COL,), K // 3, K + 1, dtype=jnp.int32)
    chosen = jax.random.randint(second, (), 0, N_ROW * N_COL, dtype=jnp.int32)
    counts = counts.at[chosen].set(K)
    return counts.reshape(N_ROW, N_COL).astype(jnp.int32)


def block_levels(stream_key, dims, cuts, smallest, largest):
    level = 1.0
    for dim, parts in cuts:
        draws = jax.random.uniform(jax.random.fold_in(jax.random.fold_in(stream_key, 6), dim), (parts,), jnp.float32, smallest / len(cuts), largest / len(cuts))
        level = level * jnp.repeat(jnp.exp(draws), dims[dim] // parts).reshape((-1,) + (1,) * (len(dims) - 1 - dim))
    return level


def gaussian(stream_key, extent, scale, limit, cuts=(), kind=jnp.bfloat16):
    array = scale * jax.random.normal(stream_key, extent, jnp.float32)
    if cuts:
        array = array * block_levels(stream_key, extent, cuts, -0.22, 0.18)
    return jnp.clip(array, -limit, limit).astype(kind)


def setup_inputs(seed: int = 0) -> dict:
    key_of = jax.random.split(jax.random.key(seed), 8)
    return {
        "user_factors": gaussian(key_of[0], (USERS, R), 0.25, 4.0, ((0, 32),)),
        "item_factors": gaussian(key_of[1], (ITEMS, R), 0.25, 4.0, ((0, 32),)),
        "start_vectors": gaussian(key_of[2], (ITEMS, VECS), 1.0, 6.0, ((0, 32),)),
        "ratings": gaussian(key_of[3], (N_ROW, N_COL, K, TILE, TILE), 1.0, 6.0, ((0, 4), (1, 8))),
        "tile_rows": draw_tile_rows(jax.random.fold_in(key_of[7], 71), 0),
        "tile_cols": draw_tile_cols(jax.random.fold_in(key_of[7], 71), 0),
        "tile_count": draw_tile_count(jax.random.fold_in(key_of[7], 71), 0),
    }


def device_residual(user_tiles, item_tiles, rating, rows, cols, valid):
    left = user_tiles[rows].astype(jnp.float32)
    right = item_tiles[cols].astype(jnp.float32)
    product = jnp.einsum('kir,kjr->kij', left, right)
    res = (product - rating.astype(jnp.float32)) * valid[:, None, None]
    return res.astype(jnp.bfloat16)

def orthonormal(block):
    gram = jnp.dot(block.T.astype(jnp.float32), block.astype(jnp.float32), precision=lax.Precision.HIGHEST, preferred_element_type=jnp.float32)
    lower = jnp.linalg.cholesky(gram)
    return lax.linalg.triangular_solve(lower, block, left_side=False, lower=True, transpose_a=True)

def reference(user_factors, item_factors, start_vectors, ratings, tile_rows, tile_cols, tile_count):
    user_tiles = user_factors.reshape(USERS // TILE, TILE, R)
    item_tiles = item_factors.reshape(ITEMS // TILE, TILE, R)
    slots = jnp.arange(K, dtype=jnp.int32)

    def device_data(index):
        rdev = index // N_COL
        cdev = index % N_COL
        rows = (tile_rows[rdev, cdev] + rdev * TU).astype(jnp.int32)
        cols = (tile_cols[rdev, cdev] + cdev * TI).astype(jnp.int32)
        valid = (slots < tile_count[rdev, cdev]).astype(jnp.float32)
        res = device_residual(user_tiles, item_tiles, ratings[rdev, cdev], rows, cols, valid)
        return (res, rows, cols)

    def forward(basis):
        basis_tiles = basis.reshape(ITEMS // TILE, TILE, VECS)

        def step(total, index):
            res, rows, cols = device_data(index)
            contrib = jnp.einsum('kij,kjc->kic', res.astype(jnp.float32), basis_tiles[cols].astype(jnp.float32))
            return (total.at[rows].add(contrib), None)
        start = jnp.zeros((USERS // TILE, TILE, VECS), jnp.float32)
        total, _ = lax.scan(step, start, jnp.arange(N_ROW * N_COL, dtype=jnp.int32))
        return total.reshape(USERS, VECS)

    def backward(basis):
        basis_tiles = basis.reshape(USERS // TILE, TILE, VECS)

        def step(total, index):
            res, rows, cols = device_data(index)
            contrib = jnp.einsum('kij,kic->kjc', res.astype(jnp.float32), basis_tiles[rows].astype(jnp.float32))
            return (total.at[cols].add(contrib), None)
        start = jnp.zeros((ITEMS // TILE, TILE, VECS), jnp.float32)
        total, _ = lax.scan(step, start, jnp.arange(N_ROW * N_COL, dtype=jnp.int32))
        return total.reshape(ITEMS, VECS)
    basis_items = start_vectors
    for step_index in range(2):
        users_q = orthonormal(forward(basis_items))
        user_basis = users_q.astype(jnp.bfloat16)
        items_p = orthonormal(backward(user_basis))
        basis_items = items_p.astype(jnp.bfloat16)
    return (users_q * jnp.sqrt(jnp.float32(USERS)), items_p * jnp.sqrt(jnp.float32(ITEMS)))
```

```python
import functools

import jax
import jax.numpy as jnp
from jax import lax
from jax.experimental import pallas as pl
from jax.experimental.pallas import tpu as pltpu
from jax.sharding import PartitionSpec as P

MESH = pl.DeviceIdType.MESH
HIGHEST = lax.Precision.HIGHEST
ITERS = 2
UNROLL = 4


def aligned(index, size):
    return pl.ds(pl.multiple_of(index * size, size), size)


class Group:
    def __init__(self, axis, size, other_axis):
        self.axis = axis
        self.size = size
        self.outer = size // 2
        self.me = lax.axis_index(axis)
        self.other = lax.axis_index(other_axis)
        self.o = self.me // 2
        self.i = self.me % 2

    def device(self, index):
        if self.axis == "col":
            return (self.other, index)
        return (index, self.other)

    def ahead(self, t):
        return (self.o + t) % self.outer

    def behind(self, t):
        return (self.o + self.outer - t) % self.outer


def remote(src, dst, send, recv, device):
    return pltpu.make_async_remote_copy(
        src_ref=src, dst_ref=dst, send_sem=send, recv_sem=recv, device_id=device, device_id_type=MESH
    )


class Gather:
    def __init__(self, group, full, sems):
        self.group, self.full = group, full
        self.outer_send, self.outer_recv, self.inner_send, self.inner_recv = sems

    def outer_copy(self, t):
        g = self.group
        block = self.full.at[g.me]
        return remote(
            block, block, self.outer_send.at[t], self.outer_recv.at[t], g.device(g.ahead(t) * 2 + g.i)
        )

    def outer_arrival(self, t):
        g = self.group
        block = self.full.at[g.behind(t) * 2 + g.i]
        return remote(
            block, block, self.outer_send.at[t], self.outer_recv.at[t], g.device(g.ahead(t) * 2 + g.i)
        )

    def inner_copy(self, t):
        g = self.group
        block = self.full.at[g.behind(t) * 2 + g.i]
        return remote(
            block, block, self.inner_send.at[t], self.inner_recv.at[t], g.device(g.o * 2 + 1 - g.i)
        )

    def inner_arrival(self, t):
        g = self.group
        block = self.full.at[g.behind(t) * 2 + 1 - g.i]
        return remote(
            block, block, self.inner_send.at[t], self.inner_recv.at[t], g.device(g.o * 2 + 1 - g.i)
        )

    def start(self):
        for t in range(self.group.outer - 1, 0, -1):
            self.outer_copy(t).start()
        self.inner_copy(0).start()

    def forward(self, t):
        self.outer_arrival(t).wait_recv()
        self.inner_copy(t).start()

    def finish(self):
        for t in range(1, self.group.outer):
            self.forward(t)
        for t in range(self.group.outer):
            self.inner_arrival(t).wait_recv()

    def drain(self):
        for t in range(1, self.group.outer):
            self.outer_copy(t).wait_send()
        for t in range(self.group.outer):
            self.inner_copy(t).wait_send()


class Scatter:
    def __init__(self, group, own, inner_out, inner_in, outer_out, outer_in, sems):
        self.group = group
        self.own, self.inner_out, self.inner_in = own, inner_out, inner_in
        self.outer_out, self.outer_in = outer_out, outer_in
        self.outer_send, self.outer_recv, self.inner_send, self.inner_recv = sems

    def inner_copy(self, t):
        g = self.group
        return remote(
            self.inner_out.at[t],
            self.inner_in.at[t],
            self.inner_send.at[t],
            self.inner_recv.at[t],
            g.device(g.o * 2 + 1 - g.i),
        )

    def outer_copy(self, t):
        g = self.group
        return remote(
            self.outer_out.at[t],
            self.outer_in.at[t],
            self.outer_send.at[t],
            self.outer_recv.at[t],
            g.device(g.ahead(t) * 2 + g.i),
        )

    def products(self, matrix, basis):
        g = self.group
        share = self.own.shape[1]
        chunk = min(share, 256)

        def block(index, store):
            def part(h, _):
                base = pl.multiple_of(index * share + h * chunk, chunk)
                store(
                    h,
                    jnp.dot(
                        matrix[pl.ds(base, chunk), :], basis(), preferred_element_type=jnp.float32
                    ),
                )
                return 0

            lax.fori_loop(0, share // chunk, part, 0)

        def step(s, _):
            t = (s + 1) % g.outer
            there = g.ahead(t)

            def store_out(h, value):
                self.inner_out[t, aligned(h, chunk), :] = value.astype(jnp.bfloat16)

            def store_own(h, value):
                self.own[t, aligned(h, chunk), :] = value

            block(there * 2 + 1 - g.i, store_out)
            self.inner_copy(t).start()
            block(there * 2 + g.i, store_own)
            return 0

        lax.fori_loop(0, g.outer, step, 0)

    def pass_on(self):
        def step(t, _):
            self.inner_copy(t).wait_recv()
            self.outer_out[t] = (self.own[t] + self.inner_in[t].astype(jnp.float32)).astype(
                jnp.bfloat16
            )
            self.outer_copy(t).start()
            return 0

        lax.fori_loop(1, self.group.outer, step, 0)

    def total(self):
        self.inner_copy(0).wait_recv()
        self.own[0] = self.own[0] + self.inner_in[0].astype(jnp.float32)

        def step(t, _):
            self.outer_copy(t).wait_recv()
            self.own[0] = self.own[0] + self.outer_in[t].astype(jnp.float32)
            return 0

        lax.fori_loop(1, self.group.outer, step, 0)

    def drain(self):
        for t in range(1, self.group.outer):
            self.outer_copy(t).wait_send()
        for t in range(self.group.outer):
            self.inner_copy(t).wait_send()


class Gram:
    def __init__(self, row, col, parts, arrived, mine, others, full, sems):
        self.row, self.col = row, col
        self.parts, self.arrived, self.mine, self.others, self.full = parts, arrived, mine, others, full
        self.sems = sems

    def scatter_copy(self, t):
        c = self.col
        there = (c.me + t) % c.size
        return remote(
            self.parts.at[there],
            self.arrived.at[t],
            self.sems[0].at[t],
            self.sems[1].at[t],
            c.device(there),
        )

    def exchange_copy(self, t):
        r = self.row
        return remote(
            self.mine.at[0],
            self.others.at[t],
            self.sems[2].at[t],
            self.sems[3].at[t],
            r.device((r.me + t) % r.size),
        )

    def gather_copy(self, t):
        c = self.col
        return remote(
            self.full.at[c.me],
            self.full.at[c.me],
            self.sems[4].at[t],
            self.sems[5].at[t],
            c.device((c.me + t) % c.size),
        )

    def gather_arrival(self, t):
        c = self.col
        block = self.full.at[(c.me + c.size - t) % c.size]
        return remote(
            block, block, self.sems[4].at[t], self.sems[5].at[t], c.device((c.me + t) % c.size)
        )

    def begin(self, block):
        gram = lax.dot_general(
            block, block, (((0,), (0,)), ((), ())), precision=HIGHEST, preferred_element_type=jnp.float32
        )
        rows = self.parts.shape[1]
        for index in range(self.col.size):
            self.parts[index] = gram[index * rows : (index + 1) * rows, :]
        for t in range(1, self.col.size):
            self.scatter_copy(t).start()

    def exchange(self):
        for t in range(1, self.col.size):
            self.scatter_copy(t).wait_recv()
        total = self.parts[self.col.me]
        for t in range(1, self.col.size):
            total = total + self.arrived[t]
        self.mine[0] = total
        for t in range(1, self.row.size):
            self.exchange_copy(t).start()

    def spread(self):
        for t in range(1, self.row.size):
            self.exchange_copy(t).wait_recv()
        total = self.mine[0]
        for t in range(1, self.row.size):
            total = total + self.others[t]
        self.full[self.col.me] = total
        for t in range(1, self.col.size):
            self.gather_copy(t).start()

    def collect(self, work):
        for t in range(1, self.col.size):
            self.gather_arrival(t).wait_recv()
        rows = self.parts.shape[1]
        for index in range(self.col.size):
            work[index * rows : (index + 1) * rows, :] = self.full[index]

    def drain(self):
        for t in range(1, self.col.size):
            self.scatter_copy(t).wait_send()
            self.gather_copy(t).wait_send()
        for t in range(1, self.row.size):
            self.exchange_copy(t).wait_send()


def eliminate(work):
    size = work.shape[0]
    lanes = lax.broadcasted_iota(jnp.int32, (size, size), 1)
    subs = lax.broadcasted_iota(jnp.int32, (size, size), 0)
    lane_row = lax.broadcasted_iota(jnp.int32, (1, size), 1)

    def step(j, _):
        matrix = work[...]
        row = work[pl.ds(j, 1), :]
        pivot = jnp.sum(jnp.where(lane_row == j, row, 0.0), axis=1, keepdims=True)
        scaled = jnp.where(lane_row == j, 1.0, row) / pivot
        here = lanes == j
        column = jnp.sum(jnp.where(here & (subs > j), matrix, 0.0), axis=1, keepdims=True)
        kept = jnp.where(here & (subs > j), 0.0, matrix)
        work[...] = kept - column * scaled
        return 0

    lax.fori_loop(0, size, step, 0)


def inverse_factor(work):
    size = work.shape[0]
    lanes = lax.broadcasted_iota(jnp.int32, (size, size), 1)
    subs = lax.broadcasted_iota(jnp.int32, (size, size), 0)
    matrix = work[...]
    pivots = jnp.sum(jnp.where(lanes == subs, matrix, 0.0), axis=1, keepdims=True)
    unit = jnp.where(lanes == subs, 1.0, jnp.where(lanes < subs, matrix, 0.0))
    return unit * lax.rsqrt(pivots)


def times_transposed(block, inverse):
    return lax.dot_general(
        block, inverse, (((1,), (1,)), ((), ())), precision=HIGHEST, preferred_element_type=jnp.float32
    )


def kernel(n_row, n_col, *refs):
    refs = list(refs)

    def take(count):
        got = refs[:count]
        del refs[:count]
        return got

    rows, cols, slot_of, users, items, start, ratings = take(7)
    user_out, item_out = take(2)
    user_full, item_full, start_full, user_wide, item_wide, res, res_t, block, block_t, work = take(10)
    row = Group("row", n_row, "col")
    col = Group("col", n_col, "row")
    user_gather = Gather(col, user_full, take(4))
    item_gather = Gather(row, item_full, take(4))
    start_gather = Gather(row, start_full, take(4))
    forward_sums, backward_sums, user_gathers, item_gathers, grams = [], [], [], [], []
    for _ in range(ITERS):
        forward_sums.append(Scatter(col, *take(5), take(4)))
        backward_sums.append(Scatter(row, *take(5), take(4)))
        user_gathers.append(Gather(col, *take(1), take(4)))
    for _ in range(ITERS - 1):
        item_gathers.append(Gather(row, *take(1), take(4)))
    for _ in range(2 * ITERS):
        grams.append(Gram(row, col, *take(5), take(6)))
    assert not refs

    barrier = pltpu.get_barrier_semaphore()
    for group in (row, col):
        for t in range(1, group.size):
            pl.semaphore_signal(
                barrier, inc=1, device_id=group.device((group.me + t) % group.size), device_id_type=MESH
            )
    pl.semaphore_wait(barrier, n_row + n_col - 2)

    user_full[col.me] = users[...]
    user_gather.start()
    item_full[row.me] = items[...]
    item_gather.start()
    start_full[row.me] = start[...]
    start_gather.start()

    slots, tile, _ = ratings.shape
    user_tiles = block.shape[0] // tile
    item_tiles = block.shape[1] // tile
    res[slots] = jnp.zeros((tile, tile), jnp.bfloat16)
    res_t[slots] = jnp.zeros((tile, tile), jnp.bfloat16)

    item_gather.finish()
    user_gather.finish()

    half = users.shape[0]
    rank = users.shape[1] // 2
    piece = min(half, tile)
    low = lax.broadcasted_iota(jnp.int32, (piece, 2 * rank), 1) < rank

    def widen(index, _):
        for side in range(2):
            for base in range(0, half, piece):
                packed = user_full[index, base : base + piece, :].astype(jnp.float32)
                value = jnp.where(low, packed, 0.0) if side == 0 else jnp.where(low, 0.0, packed)
                place = index * 2 * half + side * half + base
                inside = pl.ds(pl.multiple_of(place % tile, piece), piece)
                user_wide[place // tile, inside, :] = value.astype(jnp.bfloat16)
        return 0

    lax.fori_loop(0, n_col, widen, 0)
    per_share = item_full.shape[1] // tile
    for index in range(n_row):
        for q in range(per_share):
            item_wide[index * per_share + q] = item_full[index, q * tile : (q + 1) * tile, :]

    def residual(s, _):
        for u in range(UNROLL):
            k = s * UNROLL + u
            left = user_wide[rows[k]]
            right = item_wide[cols[k]]
            product = lax.dot_general(
                left, right, (((1,), (1,)), ((), ())), preferred_element_type=jnp.float32
            )
            value = product - ratings[k].astype(jnp.float32)
            res[k] = value.astype(jnp.bfloat16)
            res_t[k] = value.T.astype(jnp.bfloat16)
        return 0

    lax.fori_loop(0, slots // UNROLL, residual, 0)

    def lay_row(a, _):
        for b in range(item_tiles):
            block[aligned(a, tile), b * tile : (b + 1) * tile] = res[slot_of[a * item_tiles + b]]
        return 0

    lax.fori_loop(0, user_tiles, lay_row, 0)

    def lay_column(b, _):
        for a in range(user_tiles):
            block_t[aligned(b, tile), a * tile : (a + 1) * tile] = res_t[slot_of[a * item_tiles + b]]
        return 0

    lax.fori_loop(0, item_tiles, lay_column, 0)
    start_gather.finish()

    def normalised(gram, source):
        gram.begin(source[0])
        gram.exchange()
        gram.spread()
        gram.collect(work)
        eliminate(work)
        return times_transposed(source[0], inverse_factor(work))

    def whole(full):
        return lambda: full[...].reshape(full.shape[0] * full.shape[1], full.shape[2])

    items_now = start_full
    for index in range(ITERS):
        sums = forward_sums[index]
        sums.products(block, whole(items_now))
        sums.pass_on()
        sums.total()
        basis = normalised(grams[2 * index], sums.own)
        if index == ITERS - 1:
            user_out[...] = basis
        gather = user_gathers[index]
        gather.full[col.me] = basis.astype(jnp.bfloat16)
        gather.start()
        gather.finish()
        sums = backward_sums[index]
        sums.products(block_t, whole(gather.full))
        sums.pass_on()
        sums.total()
        basis = normalised(grams[2 * index + 1], sums.own)
        if index == ITERS - 1:
            item_out[...] = basis
        else:
            gather = item_gathers[index]
            gather.full[row.me] = basis.astype(jnp.bfloat16)
            gather.start()
            gather.finish()
            items_now = gather.full

    for part in (
        [user_gather, item_gather, start_gather]
        + forward_sums
        + backward_sums
        + user_gathers
        + item_gathers
        + grams
    ):
        part.drain()


def shards(n_row, n_col, user_factors, item_factors, start_vectors, ratings, tile_rows, tile_cols, tile_count):
    slots, tile = ratings.shape[2], ratings.shape[-1]
    vecs = start_vectors.shape[1]
    users_share, rank = user_factors.shape
    items_share = item_factors.shape[0]
    users_block, items_block = users_share * n_col, items_share * n_row
    user_tiles, item_tiles = users_block // tile, items_block // tile
    rows, cols = tile_rows[0, 0], tile_cols[0, 0]
    number = jnp.arange(slots, dtype=jnp.int32)
    names = jnp.where(number < tile_count[0, 0], rows * item_tiles + cols, -1)
    places = jnp.arange(user_tiles * item_tiles, dtype=jnp.int32)
    slot_of = slots + jnp.sum(
        jnp.where(names[None, :] == places[:, None], number[None, :] - slots, 0), axis=1
    )
    half = users_share // 2
    users = jnp.concatenate([user_factors[:half], user_factors[half:]], axis=1)
    items = jnp.concatenate([item_factors, item_factors], axis=1)

    bf16, f32 = jnp.bfloat16, jnp.float32
    dma = pltpu.SemaphoreType.DMA

    def gather_sems(size):
        return [dma((size // 2,))] * 4

    def scatter_scratch(size, share):
        outer = size // 2
        return [
            pltpu.VMEM((outer, share, vecs), f32),
            pltpu.VMEM((outer, share, vecs), bf16),
            pltpu.VMEM((outer, share, vecs), bf16),
            pltpu.VMEM((outer, share, vecs), bf16),
            pltpu.VMEM((outer, share, vecs), bf16),
        ] + gather_sems(size)

    scratch = [
        pltpu.VMEM((n_col, half, 2 * rank), bf16),
        pltpu.VMEM((n_row, items_share, 2 * rank), bf16),
        pltpu.VMEM((n_row, items_share, vecs), bf16),
        pltpu.VMEM((user_tiles, tile, 2 * rank), bf16),
        pltpu.VMEM((item_tiles, tile, 2 * rank), bf16),
        pltpu.VMEM((slots + 1, tile, tile), bf16),
        pltpu.VMEM((slots + 1, tile, tile), bf16),
        pltpu.VMEM((users_block, items_block), bf16),
        pltpu.VMEM((items_block, users_block), bf16),
        pltpu.VMEM((vecs, vecs), f32),
    ]
    scratch += gather_sems(n_col) + gather_sems(n_row) + gather_sems(n_row)
    for _ in range(ITERS):
        scratch += scatter_scratch(n_col, users_share)
        scratch += scatter_scratch(n_row, items_share)
        scratch += [pltpu.VMEM((n_col, users_share, vecs), bf16)] + gather_sems(n_col)
    for _ in range(ITERS - 1):
        scratch += [pltpu.VMEM((n_row, items_share, vecs), bf16)] + gather_sems(n_row)
    for _ in range(2 * ITERS):
        part = vecs // n_col
        scratch += [
            pltpu.VMEM((n_col, part, vecs), f32),
            pltpu.VMEM((n_col, part, vecs), f32),
            pltpu.VMEM((1, part, vecs), f32),
            pltpu.VMEM((n_row, part, vecs), f32),
            pltpu.VMEM((n_col, part, vecs), f32),
        ]
        scratch += [dma((n_col,)), dma((n_col,)), dma((n_row,)), dma((n_row,)), dma((n_col,)), dma((n_col,))]

    smem, vmem = pl.BlockSpec(memory_space=pltpu.SMEM), pl.BlockSpec(memory_space=pltpu.VMEM)
    user_basis, item_basis = pl.pallas_call(
        functools.partial(kernel, n_row, n_col),
        out_shape=(
            jax.ShapeDtypeStruct((users_share, vecs), f32),
            jax.ShapeDtypeStruct((items_share, vecs), f32),
        ),
        in_specs=[smem] * 3 + [vmem] * 4,
        out_specs=(vmem, vmem),
        scratch_shapes=scratch,
        compiler_params=pltpu.CompilerParams(
            collective_id=0, has_side_effects=True, vmem_limit_bytes=62 * 1024 * 1024
        ),
    )(rows, cols, slot_of, users, items, start_vectors, ratings[0, 0])
    users_total = users_share * n_row * n_col
    items_total = items_share * n_row * n_col
    return (
        user_basis * jnp.sqrt(jnp.float32(users_total)),
        item_basis * jnp.sqrt(jnp.float32(items_total)),
    )


def solution(mesh):
    in_specs = (
        P(("row", "col"), None),
        P(("col", "row"), None),
        P(("col", "row"), None),
        P("row", "col", None, None, None),
        P("row", "col", None),
        P("row", "col", None),
        P("row", "col"),
    )
    out_specs = (P(("row", "col"), None), P(("col", "row"), None))
    body = functools.partial(shards, mesh.shape["row"], mesh.shape["col"])
    return jax.shard_map(body, mesh=mesh, in_specs=in_specs, out_specs=out_specs, check_vma=False)
```

```python
import functools

import jax
import jax.numpy as jnp
from jax import lax
from jax.experimental import pallas as pl
from jax.experimental.pallas import tpu as pltpu
from jax.sharding import PartitionSpec as P

MESH = pl.DeviceIdType.MESH
HIGHEST = lax.Precision.HIGHEST
ITERS = 2
UNROLL = 4
PANEL = 32
SUB = 8


def aligned(index, size):
    return pl.ds(pl.multiple_of(index * size, size), size)


class Group:
    def __init__(self, axis, size, other_axis):
        self.axis = axis
        self.size = size
        self.outer = size // 2
        self.me = lax.axis_index(axis)
        self.other = lax.axis_index(other_axis)
        self.o = self.me // 2
        self.i = self.me % 2

    def device(self, index):
        if self.axis == "col":
            return (self.other, index)
        return (index, self.other)

    def ahead(self, t):
        return (self.o + t) % self.outer

    def behind(self, t):
        return (self.o + self.outer - t) % self.outer


def remote(src, dst, send, recv, device):
    return pltpu.make_async_remote_copy(
        src_ref=src, dst_ref=dst, send_sem=send, recv_sem=recv, device_id=device, device_id_type=MESH
    )


class Gather:
    def __init__(self, group, full, sems):
        self.group, self.full = group, full
        self.outer_send, self.outer_recv, self.inner_send, self.inner_recv = sems

    def outer_copy(self, t):
        g = self.group
        block = self.full.at[g.me]
        return remote(
            block, block, self.outer_send.at[t], self.outer_recv.at[t], g.device(g.ahead(t) * 2 + g.i)
        )

    def outer_arrival(self, t):
        g = self.group
        block = self.full.at[g.behind(t) * 2 + g.i]
        return remote(
            block, block, self.outer_send.at[t], self.outer_recv.at[t], g.device(g.ahead(t) * 2 + g.i)
        )

    def inner_copy(self, t):
        g = self.group
        block = self.full.at[g.behind(t) * 2 + g.i]
        return remote(
            block, block, self.inner_send.at[t], self.inner_recv.at[t], g.device(g.o * 2 + 1 - g.i)
        )

    def inner_arrival(self, t):
        g = self.group
        block = self.full.at[g.behind(t) * 2 + 1 - g.i]
        return remote(
            block, block, self.inner_send.at[t], self.inner_recv.at[t], g.device(g.o * 2 + 1 - g.i)
        )

    def start(self):
        for t in range(self.group.outer - 1, 0, -1):
            self.outer_copy(t).start()
        self.inner_copy(0).start()

    def forward(self, t):
        self.outer_arrival(t).wait_recv()
        self.inner_copy(t).start()

    def finish(self):
        for t in range(1, self.group.outer):
            self.forward(t)
        for t in range(self.group.outer):
            self.inner_arrival(t).wait_recv()

    def drain(self):
        for t in range(1, self.group.outer):
            self.outer_copy(t).wait_send()
        for t in range(self.group.outer):
            self.inner_copy(t).wait_send()


class Scatter:
    def __init__(self, group, own, inner_out, inner_in, outer_out, outer_in, sems):
        self.group = group
        self.own, self.inner_out, self.inner_in = own, inner_out, inner_in
        self.outer_out, self.outer_in = outer_out, outer_in
        self.outer_send, self.outer_recv, self.inner_send, self.inner_recv = sems

    def inner_copy(self, t):
        g = self.group
        return remote(
            self.inner_out.at[t],
            self.inner_in.at[t],
            self.inner_send.at[t],
            self.inner_recv.at[t],
            g.device(g.o * 2 + 1 - g.i),
        )

    def outer_copy(self, t):
        g = self.group
        return remote(
            self.outer_out.at[t],
            self.outer_in.at[t],
            self.outer_send.at[t],
            self.outer_recv.at[t],
            g.device(g.ahead(t) * 2 + g.i),
        )

    def products(self, matrix, basis):
        g = self.group
        share = self.own.shape[1]
        chunk = min(share, 256)

        def block(index, store):
            def part(h, _):
                base = pl.multiple_of(index * share + h * chunk, chunk)
                store(
                    h,
                    jnp.dot(
                        matrix[pl.ds(base, chunk), :], basis(), preferred_element_type=jnp.float32
                    ),
                )
                return 0

            lax.fori_loop(0, share // chunk, part, 0)

        def step(s, _):
            t = (s + 1) % g.outer
            there = g.ahead(t)

            def store_out(h, value):
                self.inner_out[t, aligned(h, chunk), :] = value.astype(jnp.bfloat16)

            def store_own(h, value):
                self.own[t, aligned(h, chunk), :] = value

            block(there * 2 + 1 - g.i, store_out)
            self.inner_copy(t).start()
            block(there * 2 + g.i, store_own)
            return 0

        lax.fori_loop(0, g.outer, step, 0)

    def pass_on(self):
        def step(t, _):
            self.inner_copy(t).wait_recv()
            self.outer_out[t] = (self.own[t] + self.inner_in[t].astype(jnp.float32)).astype(
                jnp.bfloat16
            )
            self.outer_copy(t).start()
            return 0

        lax.fori_loop(1, self.group.outer, step, 0)

    def total(self):
        self.inner_copy(0).wait_recv()
        self.own[0] = self.own[0] + self.inner_in[0].astype(jnp.float32)

        def step(t, _):
            self.outer_copy(t).wait_recv()
            self.own[0] = self.own[0] + self.outer_in[t].astype(jnp.float32)
            return 0

        lax.fori_loop(1, self.group.outer, step, 0)

    def drain(self):
        for t in range(1, self.group.outer):
            self.outer_copy(t).wait_send()
        for t in range(self.group.outer):
            self.inner_copy(t).wait_send()


class Gram:
    def __init__(self, row, col, parts, arrived, mine, others, full, sems):
        self.row, self.col = row, col
        self.parts, self.arrived, self.mine, self.others, self.full = parts, arrived, mine, others, full
        self.sems = sems

    def scatter_copy(self, t):
        c = self.col
        there = (c.me + t) % c.size
        return remote(
            self.parts.at[there],
            self.arrived.at[t],
            self.sems[0].at[t],
            self.sems[1].at[t],
            c.device(there),
        )

    def exchange_copy(self, t):
        r = self.row
        return remote(
            self.mine.at[0],
            self.others.at[t],
            self.sems[2].at[t],
            self.sems[3].at[t],
            r.device((r.me + t) % r.size),
        )

    def gather_copy(self, t):
        c = self.col
        return remote(
            self.full.at[c.me],
            self.full.at[c.me],
            self.sems[4].at[t],
            self.sems[5].at[t],
            c.device((c.me + t) % c.size),
        )

    def gather_arrival(self, t):
        c = self.col
        block = self.full.at[(c.me + c.size - t) % c.size]
        return remote(
            block, block, self.sems[4].at[t], self.sems[5].at[t], c.device((c.me + t) % c.size)
        )

    def begin(self, block):
        gram = lax.dot_general(
            block, block, (((0,), (0,)), ((), ())), precision=HIGHEST, preferred_element_type=jnp.float32
        )
        rows = self.parts.shape[1]
        for index in range(self.col.size):
            self.parts[index] = gram[index * rows : (index + 1) * rows, :]
        for t in range(1, self.col.size):
            self.scatter_copy(t).start()

    def exchange(self):
        for t in range(1, self.col.size):
            self.scatter_copy(t).wait_recv()
        total = self.parts[self.col.me]
        for t in range(1, self.col.size):
            total = total + self.arrived[t]
        self.mine[0] = total
        for t in range(1, self.row.size):
            self.exchange_copy(t).start()

    def spread(self):
        for t in range(1, self.row.size):
            self.exchange_copy(t).wait_recv()
        total = self.mine[0]
        for t in range(1, self.row.size):
            total = total + self.others[t]
        self.full[self.col.me] = total
        for t in range(1, self.col.size):
            self.gather_copy(t).start()

    def collect(self, work):
        for t in range(1, self.col.size):
            self.gather_arrival(t).wait_recv()
        rows = self.parts.shape[1]
        for index in range(self.col.size):
            work[index * rows : (index + 1) * rows, :] = self.full[index]

    def drain(self):
        for t in range(1, self.col.size):
            self.scatter_copy(t).wait_send()
            self.gather_copy(t).wait_send()
        for t in range(1, self.row.size):
            self.exchange_copy(t).wait_send()


def eliminate(work, panel):
    size = work.shape[0]
    base = pl.multiple_of(panel * PANEL, PANEL)
    lanes = lax.broadcasted_iota(jnp.int32, (PANEL, size), 1)
    subs = lax.broadcasted_iota(jnp.int32, (PANEL, size), 0)
    done, active = [], work[pl.ds(base, PANEL), :]
    for q in range(PANEL // SUB):
        lane, sub = lanes[q * SUB :], subs[: PANEL - q * SUB]
        columns = []
        for b in range(SUB):
            picked = jnp.where(lane == base + q * SUB + b, active, 0.0)
            columns.append(jnp.broadcast_to(jnp.sum(picked, axis=1, keepdims=True), active.shape))
        for a in range(SUB):
            here = lane == base + q * SUB + a
            inverse = 1.0 / columns[a][a : a + 1, :]
            factor = jnp.where(sub > a, columns[a] * inverse, 0.0)
            row = jnp.where(here[:1], 1.0, active[a : a + 1, :])
            active = jnp.where(here & (sub > a), 0.0, active) - factor * row
            for b in range(a + 1, SUB):
                columns[b] = columns[b] - factor * columns[b][a : a + 1, :]
        done.append(active[:SUB])
        active = active[SUB:]
    rows = jnp.concatenate(done, axis=0)
    work[pl.ds(base, PANEL), :] = rows
    diagonal = lanes == base + subs
    pivots = jnp.sum(jnp.where(diagonal, rows, 0.0), axis=1, keepdims=True)
    inside = (lanes >= base) & (lanes < base + PANEL)
    factors = jnp.where(lanes >= base + PANEL, rows, 0.0) / pivots
    full = jnp.where(inside & (lanes > base + subs), 0.0, jnp.where(diagonal, 1.0, rows))
    update = lax.dot_general(
        factors, full, (((0,), (0,)), ((), ())), precision=HIGHEST, preferred_element_type=jnp.float32
    )
    lane = lax.broadcasted_iota(jnp.int32, (size, size), 1)
    sub = lax.broadcasted_iota(jnp.int32, (size, size), 0)
    fresh = (lane >= base) & (lane < base + PANEL) & (sub >= base + PANEL)
    work[...] = jnp.where(fresh, 0.0, work[...]) - update


def inverse_factor(work):
    size = work.shape[0]
    lanes = lax.broadcasted_iota(jnp.int32, (size, size), 1)
    subs = lax.broadcasted_iota(jnp.int32, (size, size), 0)
    matrix = work[...]
    pivots = jnp.sum(jnp.where(lanes == subs, matrix, 0.0), axis=1, keepdims=True)
    unit = jnp.where(lanes == subs, 1.0, jnp.where(lanes < subs, matrix, 0.0))
    return unit * lax.rsqrt(pivots)


def times_transposed(block, inverse):
    return lax.dot_general(
        block, inverse, (((1,), (1,)), ((), ())), precision=HIGHEST, preferred_element_type=jnp.float32
    )


def kernel(n_row, n_col, *refs):
    refs = list(refs)

    def take(count):
        got = refs[:count]
        del refs[:count]
        return got

    rows, cols, slot_of, users, items, start, ratings = take(7)
    user_out, item_out = take(2)
    user_full, item_full, start_full, user_wide, item_wide, res, res_t, block, block_t, work = take(10)
    row = Group("row", n_row, "col")
    col = Group("col", n_col, "row")
    user_gather = Gather(col, user_full, take(4))
    item_gather = Gather(row, item_full, take(4))
    start_gather = Gather(row, start_full, take(4))
    forward_sums, backward_sums, user_gathers, item_gathers, grams = [], [], [], [], []
    for _ in range(ITERS):
        forward_sums.append(Scatter(col, *take(5), take(4)))
        backward_sums.append(Scatter(row, *take(5), take(4)))
        user_gathers.append(Gather(col, *take(1), take(4)))
    for _ in range(ITERS - 1):
        item_gathers.append(Gather(row, *take(1), take(4)))
    for _ in range(2 * ITERS):
        grams.append(Gram(row, col, *take(5), take(6)))
    assert not refs

    barrier = pltpu.get_barrier_semaphore()
    for group in (row, col):
        for t in range(1, group.size):
            pl.semaphore_signal(
                barrier, inc=1, device_id=group.device((group.me + t) % group.size), device_id_type=MESH
            )
    pl.semaphore_wait(barrier, n_row + n_col - 2)

    user_full[col.me] = users[...]
    user_gather.start()
    item_full[row.me] = items[...]
    item_gather.start()
    start_full[row.me] = start[...]
    start_gather.start()

    slots, tile, _ = ratings.shape
    user_tiles = block.shape[0] // tile
    item_tiles = block.shape[1] // tile
    res[slots] = jnp.zeros((tile, tile), jnp.bfloat16)
    res_t[slots] = jnp.zeros((tile, tile), jnp.bfloat16)

    item_gather.finish()
    user_gather.finish()

    half = users.shape[0]
    rank = users.shape[1] // 2
    piece = min(half, tile)
    low = lax.broadcasted_iota(jnp.int32, (piece, 2 * rank), 1) < rank

    def widen(index, _):
        for side in range(2):
            for base in range(0, half, piece):
                packed = user_full[index, base : base + piece, :].astype(jnp.float32)
                value = jnp.where(low, packed, 0.0) if side == 0 else jnp.where(low, 0.0, packed)
                place = index * 2 * half + side * half + base
                inside = pl.ds(pl.multiple_of(place % tile, piece), piece)
                user_wide[place // tile, inside, :] = value.astype(jnp.bfloat16)
        return 0

    lax.fori_loop(0, n_col, widen, 0)
    per_share = item_full.shape[1] // tile
    for index in range(n_row):
        for q in range(per_share):
            item_wide[index * per_share + q] = item_full[index, q * tile : (q + 1) * tile, :]

    def residual(s, _):
        for u in range(UNROLL):
            k = s * UNROLL + u
            left = user_wide[rows[k]]
            right = item_wide[cols[k]]
            product = lax.dot_general(
                left, right, (((1,), (1,)), ((), ())), preferred_element_type=jnp.float32
            )
            value = product - ratings[k].astype(jnp.float32)
            res[k] = value.astype(jnp.bfloat16)
            res_t[k] = value.T.astype(jnp.bfloat16)
        return 0

    lax.fori_loop(0, slots // UNROLL, residual, 0)

    def lay_row(a, _):
        for b in range(item_tiles):
            block[aligned(a, tile), b * tile : (b + 1) * tile] = res[slot_of[a * item_tiles + b]]
        return 0

    lax.fori_loop(0, user_tiles, lay_row, 0)

    def lay_column(b, _):
        for a in range(user_tiles):
            block_t[aligned(b, tile), a * tile : (a + 1) * tile] = res_t[slot_of[a * item_tiles + b]]
        return 0

    lax.fori_loop(0, item_tiles, lay_column, 0)
    start_gather.finish()

    def normalised(gram, source):
        gram.begin(source[0])
        gram.exchange()
        gram.spread()
        gram.collect(work)

        def panel(index, _):
            eliminate(work, index)
            return 0

        lax.fori_loop(0, work.shape[0] // PANEL, panel, 0)
        return times_transposed(source[0], inverse_factor(work))

    def whole(full):
        return lambda: full[...].reshape(full.shape[0] * full.shape[1], full.shape[2])

    items_now = start_full
    for index in range(ITERS):
        sums = forward_sums[index]
        sums.products(block, whole(items_now))
        sums.pass_on()
        sums.total()
        basis = normalised(grams[2 * index], sums.own)
        if index == ITERS - 1:
            user_out[...] = basis
        gather = user_gathers[index]
        gather.full[col.me] = basis.astype(jnp.bfloat16)
        gather.start()
        gather.finish()
        sums = backward_sums[index]
        sums.products(block_t, whole(gather.full))
        sums.pass_on()
        sums.total()
        basis = normalised(grams[2 * index + 1], sums.own)
        if index == ITERS - 1:
            item_out[...] = basis
        else:
            gather = item_gathers[index]
            gather.full[row.me] = basis.astype(jnp.bfloat16)
            gather.start()
            gather.finish()
            items_now = gather.full

    for part in (
        [user_gather, item_gather, start_gather]
        + forward_sums
        + backward_sums
        + user_gathers
        + item_gathers
        + grams
    ):
        part.drain()


def shards(n_row, n_col, user_factors, item_factors, start_vectors, ratings, tile_rows, tile_cols, tile_count):
    slots, tile = ratings.shape[2], ratings.shape[-1]
    vecs = start_vectors.shape[1]
    users_share, rank = user_factors.shape
    items_share = item_factors.shape[0]
    users_block, items_block = users_share * n_col, items_share * n_row
    user_tiles, item_tiles = users_block // tile, items_block // tile
    rows, cols = tile_rows[0, 0], tile_cols[0, 0]
    number = jnp.arange(slots, dtype=jnp.int32)
    names = jnp.where(number < tile_count[0, 0], rows * item_tiles + cols, -1)
    places = jnp.arange(user_tiles * item_tiles, dtype=jnp.int32)
    slot_of = slots + jnp.sum(
        jnp.where(names[None, :] == places[:, None], number[None, :] - slots, 0), axis=1
    )
    half = users_share // 2
    users = jnp.concatenate([user_factors[:half], user_factors[half:]], axis=1)
    items = jnp.concatenate([item_factors, item_factors], axis=1)

    bf16, f32 = jnp.bfloat16, jnp.float32
    dma = pltpu.SemaphoreType.DMA

    def gather_sems(size):
        return [dma((size // 2,))] * 4

    def scatter_scratch(size, share):
        outer = size // 2
        return [
            pltpu.VMEM((outer, share, vecs), f32),
            pltpu.VMEM((outer, share, vecs), bf16),
            pltpu.VMEM((outer, share, vecs), bf16),
            pltpu.VMEM((outer, share, vecs), bf16),
            pltpu.VMEM((outer, share, vecs), bf16),
        ] + gather_sems(size)

    scratch = [
        pltpu.VMEM((n_col, half, 2 * rank), bf16),
        pltpu.VMEM((n_row, items_share, 2 * rank), bf16),
        pltpu.VMEM((n_row, items_share, vecs), bf16),
        pltpu.VMEM((user_tiles, tile, 2 * rank), bf16),
        pltpu.VMEM((item_tiles, tile, 2 * rank), bf16),
        pltpu.VMEM((slots + 1, tile, tile), bf16),
        pltpu.VMEM((slots + 1, tile, tile), bf16),
        pltpu.VMEM((users_block, items_block), bf16),
        pltpu.VMEM((items_block, users_block), bf16),
        pltpu.VMEM((vecs, vecs), f32),
    ]
    scratch += gather_sems(n_col) + gather_sems(n_row) + gather_sems(n_row)
    for _ in range(ITERS):
        scratch += scatter_scratch(n_col, users_share)
        scratch += scatter_scratch(n_row, items_share)
        scratch += [pltpu.VMEM((n_col, users_share, vecs), bf16)] + gather_sems(n_col)
    for _ in range(ITERS - 1):
        scratch += [pltpu.VMEM((n_row, items_share, vecs), bf16)] + gather_sems(n_row)
    for _ in range(2 * ITERS):
        part = vecs // n_col
        scratch += [
            pltpu.VMEM((n_col, part, vecs), f32),
            pltpu.VMEM((n_col, part, vecs), f32),
            pltpu.VMEM((1, part, vecs), f32),
            pltpu.VMEM((n_row, part, vecs), f32),
            pltpu.VMEM((n_col, part, vecs), f32),
        ]
        scratch += [dma((n_col,)), dma((n_col,)), dma((n_row,)), dma((n_row,)), dma((n_col,)), dma((n_col,))]

    smem, vmem = pl.BlockSpec(memory_space=pltpu.SMEM), pl.BlockSpec(memory_space=pltpu.VMEM)
    user_basis, item_basis = pl.pallas_call(
        functools.partial(kernel, n_row, n_col),
        out_shape=(
            jax.ShapeDtypeStruct((users_share, vecs), f32),
            jax.ShapeDtypeStruct((items_share, vecs), f32),
        ),
        in_specs=[smem] * 3 + [vmem] * 4,
        out_specs=(vmem, vmem),
        scratch_shapes=scratch,
        compiler_params=pltpu.CompilerParams(
            collective_id=0, has_side_effects=True, vmem_limit_bytes=62 * 1024 * 1024
        ),
    )(rows, cols, slot_of, users, items, start_vectors, ratings[0, 0])
    users_total = users_share * n_row * n_col
    items_total = items_share * n_row * n_col
    return (
        user_basis * jnp.sqrt(jnp.float32(users_total)),
        item_basis * jnp.sqrt(jnp.float32(items_total)),
    )


def solution(mesh):
    in_specs = (
        P(("row", "col"), None),
        P(("col", "row"), None),
        P(("col", "row"), None),
        P("row", "col", None, None, None),
        P("row", "col", None),
        P("row", "col", None),
        P("row", "col"),
    )
    out_specs = (P(("row", "col"), None), P(("col", "row"), None))
    body = functools.partial(shards, mesh.shape["row"], mesh.shape["col"])
    return jax.shard_map(body, mesh=mesh, in_specs=in_specs, out_specs=out_specs, check_vma=False)
```

```python
import functools

import jax
import jax.numpy as jnp
from jax import lax
from jax.experimental import pallas as pl
from jax.experimental.pallas import tpu as pltpu
from jax.sharding import PartitionSpec as P

MESH = pl.DeviceIdType.MESH
HIGHEST = lax.Precision.HIGHEST
ITERS = 2
UNROLL = 4
PANEL = 32
SUB = 8


def aligned(index, size):
    return pl.ds(pl.multiple_of(index * size, size), size)


class Group:
    def __init__(self, axis, size, other_axis):
        self.axis = axis
        self.size = size
        self.outer = size // 2
        self.me = lax.axis_index(axis)
        self.other = lax.axis_index(other_axis)
        self.o = self.me // 2
        self.i = self.me % 2

    def device(self, index):
        if self.axis == "col":
            return (self.other, index)
        return (index, self.other)

    def ahead(self, t):
        return (self.o + t) % self.outer

    def behind(self, t):
        return (self.o + self.outer - t) % self.outer


def remote(src, dst, send, recv, device):
    return pltpu.make_async_remote_copy(
        src_ref=src, dst_ref=dst, send_sem=send, recv_sem=recv, device_id=device, device_id_type=MESH
    )


class Gather:
    def __init__(self, group, full, sems):
        self.group, self.full = group, full
        self.outer_send, self.outer_recv, self.inner_send, self.inner_recv = sems

    def outer_copy(self, t):
        g = self.group
        block = self.full.at[g.me]
        return remote(
            block, block, self.outer_send.at[t], self.outer_recv.at[t], g.device(g.ahead(t) * 2 + g.i)
        )

    def outer_arrival(self, t):
        g = self.group
        block = self.full.at[g.behind(t) * 2 + g.i]
        return remote(
            block, block, self.outer_send.at[t], self.outer_recv.at[t], g.device(g.ahead(t) * 2 + g.i)
        )

    def inner_copy(self, t):
        g = self.group
        block = self.full.at[g.behind(t) * 2 + g.i]
        return remote(
            block, block, self.inner_send.at[t], self.inner_recv.at[t], g.device(g.o * 2 + 1 - g.i)
        )

    def inner_arrival(self, t):
        g = self.group
        block = self.full.at[g.behind(t) * 2 + 1 - g.i]
        return remote(
            block, block, self.inner_send.at[t], self.inner_recv.at[t], g.device(g.o * 2 + 1 - g.i)
        )

    def start(self):
        for t in range(self.group.outer - 1, 0, -1):
            self.outer_copy(t).start()
        self.inner_copy(0).start()

    def forward(self, t):
        self.outer_arrival(t).wait_recv()
        self.inner_copy(t).start()

    def finish(self):
        for t in range(1, self.group.outer):
            self.forward(t)
        self.arrivals()

    def arrivals(self):
        for t in range(self.group.outer):
            self.inner_arrival(t).wait_recv()

    def drain(self):
        for t in range(1, self.group.outer):
            self.outer_copy(t).wait_send()
        for t in range(self.group.outer):
            self.inner_copy(t).wait_send()


class Scatter:
    def __init__(self, group, own, inner_out, inner_in, outer_out, outer_in, sems):
        self.group = group
        self.own, self.inner_out, self.inner_in = own, inner_out, inner_in
        self.outer_out, self.outer_in = outer_out, outer_in
        self.outer_send, self.outer_recv, self.inner_send, self.inner_recv = sems

    def inner_copy(self, t):
        g = self.group
        return remote(
            self.inner_out.at[t],
            self.inner_in.at[t],
            self.inner_send.at[t],
            self.inner_recv.at[t],
            g.device(g.o * 2 + 1 - g.i),
        )

    def outer_copy(self, t):
        g = self.group
        return remote(
            self.outer_out.at[t],
            self.outer_in.at[t],
            self.outer_send.at[t],
            self.outer_recv.at[t],
            g.device(g.ahead(t) * 2 + g.i),
        )

    def products(self, matrix, basis):
        g = self.group
        share = self.own.shape[1]
        chunk = min(share, 256)

        def block(index, store):
            def part(h, _):
                base = pl.multiple_of(index * share + h * chunk, chunk)
                store(
                    h,
                    jnp.dot(
                        matrix[pl.ds(base, chunk), :], basis(), preferred_element_type=jnp.float32
                    ),
                )
                return 0

            lax.fori_loop(0, share // chunk, part, 0)

        def step(s, _):
            t = (s + 1) % g.outer
            there = g.ahead(t)

            def store_out(h, value):
                self.inner_out[t, aligned(h, chunk), :] = value.astype(jnp.bfloat16)

            def store_own(h, value):
                self.own[t, aligned(h, chunk), :] = value

            block(there * 2 + 1 - g.i, store_out)
            self.inner_copy(t).start()
            block(there * 2 + g.i, store_own)
            return 0

        lax.fori_loop(0, g.outer, step, 0)

    def pass_on(self, beside=None):
        def step(t, _):
            self.inner_copy(t).wait_recv()
            self.outer_out[t] = (self.own[t] + self.inner_in[t].astype(jnp.float32)).astype(
                jnp.bfloat16
            )
            self.outer_copy(t).start()
            if beside is not None:
                beside(t - 1)
            return 0

        lax.fori_loop(1, self.group.outer, step, 0)

    def total(self):
        self.inner_copy(0).wait_recv()
        self.own[0] = self.own[0] + self.inner_in[0].astype(jnp.float32)

        def step(t, _):
            self.outer_copy(t).wait_recv()
            self.own[0] = self.own[0] + self.outer_in[t].astype(jnp.float32)
            return 0

        lax.fori_loop(1, self.group.outer, step, 0)

    def drain(self):
        for t in range(1, self.group.outer):
            self.outer_copy(t).wait_send()
        for t in range(self.group.outer):
            self.inner_copy(t).wait_send()


class Gram:
    def __init__(self, row, col, parts, arrived, mine, others, full, sems):
        self.row, self.col = row, col
        self.parts, self.arrived, self.mine, self.others, self.full = parts, arrived, mine, others, full
        self.sems = sems

    def scatter_copy(self, t):
        c = self.col
        there = (c.me + t) % c.size
        return remote(
            self.parts.at[there],
            self.arrived.at[t],
            self.sems[0].at[t],
            self.sems[1].at[t],
            c.device(there),
        )

    def exchange_copy(self, t):
        r = self.row
        return remote(
            self.mine.at[0],
            self.others.at[t],
            self.sems[2].at[t],
            self.sems[3].at[t],
            r.device((r.me + t) % r.size),
        )

    def gather_copy(self, t):
        c = self.col
        return remote(
            self.full.at[c.me],
            self.full.at[c.me],
            self.sems[4].at[t],
            self.sems[5].at[t],
            c.device((c.me + t) % c.size),
        )

    def gather_arrival(self, t):
        c = self.col
        block = self.full.at[(c.me + c.size - t) % c.size]
        return remote(
            block, block, self.sems[4].at[t], self.sems[5].at[t], c.device((c.me + t) % c.size)
        )

    def begin(self, block):
        gram = lax.dot_general(
            block, block, (((0,), (0,)), ((), ())), precision=HIGHEST, preferred_element_type=jnp.float32
        )
        rows = self.parts.shape[1]
        for index in range(self.col.size):
            self.parts[index] = gram[index * rows : (index + 1) * rows, :]
        for t in range(1, self.col.size):
            self.scatter_copy(t).start()

    def exchange(self):
        for t in range(1, self.col.size):
            self.scatter_copy(t).wait_recv()
        total = self.parts[self.col.me]
        for t in range(1, self.col.size):
            total = total + self.arrived[t]
        self.mine[0] = total
        for t in range(1, self.row.size):
            self.exchange_copy(t).start()

    def spread(self):
        for t in range(1, self.row.size):
            self.exchange_copy(t).wait_recv()
        total = self.mine[0]
        for t in range(1, self.row.size):
            total = total + self.others[t]
        self.full[self.col.me] = total
        for t in range(1, self.col.size):
            self.gather_copy(t).start()

    def collect(self, work):
        for t in range(1, self.col.size):
            self.gather_arrival(t).wait_recv()
        rows = self.parts.shape[1]
        for index in range(self.col.size):
            work[index * rows : (index + 1) * rows, :] = self.full[index]

    def drain(self):
        for t in range(1, self.col.size):
            self.scatter_copy(t).wait_send()
            self.gather_copy(t).wait_send()
        for t in range(1, self.row.size):
            self.exchange_copy(t).wait_send()


def eliminate(work, panel):
    size = work.shape[0]
    base = pl.multiple_of(panel * PANEL, PANEL)
    lanes = lax.broadcasted_iota(jnp.int32, (PANEL, size), 1)
    subs = lax.broadcasted_iota(jnp.int32, (PANEL, size), 0)
    done, active = [], work[pl.ds(base, PANEL), :]
    for q in range(PANEL // SUB):
        lane, sub = lanes[q * SUB :], subs[: PANEL - q * SUB]
        columns = []
        for b in range(SUB):
            picked = jnp.where(lane == base + q * SUB + b, active, 0.0)
            columns.append(jnp.broadcast_to(jnp.sum(picked, axis=1, keepdims=True), active.shape))
        for a in range(SUB):
            here = lane == base + q * SUB + a
            inverse = 1.0 / columns[a][a : a + 1, :]
            factor = jnp.where(sub > a, columns[a] * inverse, 0.0)
            row = jnp.where(here[:1], 1.0, active[a : a + 1, :])
            active = jnp.where(here & (sub > a), 0.0, active) - factor * row
            for b in range(a + 1, SUB):
                columns[b] = columns[b] - factor * columns[b][a : a + 1, :]
        done.append(active[:SUB])
        active = active[SUB:]
    rows = jnp.concatenate(done, axis=0)
    work[pl.ds(base, PANEL), :] = rows
    diagonal = lanes == base + subs
    pivots = jnp.sum(jnp.where(diagonal, rows, 0.0), axis=1, keepdims=True)
    inside = (lanes >= base) & (lanes < base + PANEL)
    factors = jnp.where(lanes >= base + PANEL, rows, 0.0) / pivots
    full = jnp.where(inside & (lanes > base + subs), 0.0, jnp.where(diagonal, 1.0, rows))
    update = lax.dot_general(
        factors, full, (((0,), (0,)), ((), ())), precision=HIGHEST, preferred_element_type=jnp.float32
    )
    lane = lax.broadcasted_iota(jnp.int32, (size, size), 1)
    sub = lax.broadcasted_iota(jnp.int32, (size, size), 0)
    fresh = (lane >= base) & (lane < base + PANEL) & (sub >= base + PANEL)
    work[...] = jnp.where(fresh, 0.0, work[...]) - update


def inverse_factor(work):
    size = work.shape[0]
    lanes = lax.broadcasted_iota(jnp.int32, (size, size), 1)
    subs = lax.broadcasted_iota(jnp.int32, (size, size), 0)
    matrix = work[...]
    pivots = jnp.sum(jnp.where(lanes == subs, matrix, 0.0), axis=1, keepdims=True)
    unit = jnp.where(lanes == subs, 1.0, jnp.where(lanes < subs, matrix, 0.0))
    return unit * lax.rsqrt(pivots)


def times_transposed(block, inverse):
    return lax.dot_general(
        block, inverse, (((1,), (1,)), ((), ())), precision=HIGHEST, preferred_element_type=jnp.float32
    )


def kernel(n_row, n_col, *refs):
    refs = list(refs)

    def take(count):
        got = refs[:count]
        del refs[:count]
        return got

    rows, cols, slot_of, users, items, start, ratings = take(7)
    user_out, item_out = take(2)
    user_full, item_full, start_full, user_wide, item_wide, res, res_t, block, block_t, work = take(10)
    row = Group("row", n_row, "col")
    col = Group("col", n_col, "row")
    user_gather = Gather(col, user_full, take(4))
    item_gather = Gather(row, item_full, take(4))
    start_gather = Gather(row, start_full, take(4))
    forward_sums, backward_sums, user_gathers, item_gathers, grams = [], [], [], [], []
    for _ in range(ITERS):
        forward_sums.append(Scatter(col, *take(5), take(4)))
        backward_sums.append(Scatter(row, *take(5), take(4)))
        user_gathers.append(Gather(col, *take(1), take(4)))
    for _ in range(ITERS - 1):
        item_gathers.append(Gather(row, *take(1), take(4)))
    for _ in range(2 * ITERS):
        grams.append(Gram(row, col, *take(5), take(6)))
    assert not refs

    barrier = pltpu.get_barrier_semaphore()
    for group in (row, col):
        for t in range(1, group.size):
            pl.semaphore_signal(
                barrier, inc=1, device_id=group.device((group.me + t) % group.size), device_id_type=MESH
            )
    pl.semaphore_wait(barrier, n_row + n_col - 2)

    user_full[col.me] = users[...]
    user_gather.start()
    item_full[row.me] = items[...]
    item_gather.start()
    start_full[row.me] = start[...]
    start_gather.start()

    slots, tile, _ = ratings.shape
    user_tiles = block.shape[0] // tile
    item_tiles = block.shape[1] // tile
    res[slots] = jnp.zeros((tile, tile), jnp.bfloat16)
    res_t[slots] = jnp.zeros((tile, tile), jnp.bfloat16)

    item_gather.finish()
    user_gather.finish()

    half = users.shape[0]
    rank = users.shape[1] // 2
    piece = min(half, tile)
    low = lax.broadcasted_iota(jnp.int32, (piece, 2 * rank), 1) < rank

    def widen(index, _):
        for side in range(2):
            for base in range(0, half, piece):
                packed = user_full[index, base : base + piece, :].astype(jnp.float32)
                value = jnp.where(low, packed, 0.0) if side == 0 else jnp.where(low, 0.0, packed)
                place = index * 2 * half + side * half + base
                inside = pl.ds(pl.multiple_of(place % tile, piece), piece)
                user_wide[place // tile, inside, :] = value.astype(jnp.bfloat16)
        return 0

    lax.fori_loop(0, n_col, widen, 0)
    per_share = item_full.shape[1] // tile
    for index in range(n_row):
        for q in range(per_share):
            item_wide[index * per_share + q] = item_full[index, q * tile : (q + 1) * tile, :]

    def residual(s, _):
        for u in range(UNROLL):
            k = s * UNROLL + u
            left = user_wide[rows[k]]
            right = item_wide[cols[k]]
            product = lax.dot_general(
                left, right, (((1,), (1,)), ((), ())), preferred_element_type=jnp.float32
            )
            value = product - ratings[k].astype(jnp.float32)
            res[k] = value.astype(jnp.bfloat16)
            res_t[k] = value.T.astype(jnp.bfloat16)
        return 0

    lax.fori_loop(0, slots // UNROLL, residual, 0)

    def lay_row(a, _):
        for b in range(item_tiles):
            block[aligned(a, tile), b * tile : (b + 1) * tile] = res[slot_of[a * item_tiles + b]]
        return 0

    lax.fori_loop(0, user_tiles, lay_row, 0)

    def lay_column(b, _):
        for a in range(user_tiles):
            block_t[aligned(b, tile), a * tile : (a + 1) * tile] = res_t[slot_of[a * item_tiles + b]]
        return 0

    lax.fori_loop(0, item_tiles, lay_column, 0)
    start_gather.finish()

    panels = work.shape[0] // PANEL

    def eliminate_from(first):
        def panel(index, _):
            eliminate(work, index)
            return 0

        lax.fori_loop(first, panels, panel, 0)

    def whole(full):
        return lambda: full[...].reshape(full.shape[0] * full.shape[1], full.shape[2])

    def apply(sums):
        return times_transposed(sums.own[0], inverse_factor(work))

    items_now = start_full
    for index in range(ITERS):
        last = index == ITERS - 1
        sums, gram, gather = forward_sums[index], grams[2 * index], user_gathers[index]
        sums.products(block, whole(items_now))
        if index == 0:
            sums.pass_on()
            sums.total()
        else:
            beside = min(panels, col.outer - 1) if col.outer - 1 <= panels else 0
            if beside == 0:
                eliminate_from(0)
            sums.pass_on((lambda step: eliminate(work, step)) if beside else None)
            if beside:
                eliminate_from(beside)
            sums.total()
            sums.own[0] = apply(sums)
        gather.full[col.me] = sums.own[0].astype(jnp.bfloat16)
        gather.start()
        gram.begin(sums.own[0])
        gram.exchange()
        gather.forward(1)
        gram.spread()
        for t in range(2, col.outer):
            gather.forward(t)
        gram.collect(work)
        eliminate_from(0)
        if last:
            user_out[...] = apply(sums)
        gather.arrivals()
        sums, gram = backward_sums[index], grams[2 * index + 1]
        sums.products(block_t, whole(gather.full))
        sums.pass_on()
        sums.total()
        sums.own[0] = apply(sums)
        if not last:
            gather = item_gathers[index]
            gather.full[row.me] = sums.own[0].astype(jnp.bfloat16)
            gather.start()
            gram.begin(sums.own[0])
            gather.finish()
            gram.exchange()
            gram.spread()
            gram.collect(work)
            items_now = gather.full
        else:
            gram.begin(sums.own[0])
            gram.exchange()
            gram.spread()
            gram.collect(work)
            eliminate_from(0)
            item_out[...] = apply(sums)

    for part in (
        [user_gather, item_gather, start_gather]
        + forward_sums
        + backward_sums
        + user_gathers
        + item_gathers
        + grams
    ):
        part.drain()


def shards(n_row, n_col, user_factors, item_factors, start_vectors, ratings, tile_rows, tile_cols, tile_count):
    slots, tile = ratings.shape[2], ratings.shape[-1]
    vecs = start_vectors.shape[1]
    users_share, rank = user_factors.shape
    items_share = item_factors.shape[0]
    users_block, items_block = users_share * n_col, items_share * n_row
    user_tiles, item_tiles = users_block // tile, items_block // tile
    rows, cols = tile_rows[0, 0], tile_cols[0, 0]
    number = jnp.arange(slots, dtype=jnp.int32)
    names = jnp.where(number < tile_count[0, 0], rows * item_tiles + cols, -1)
    places = jnp.arange(user_tiles * item_tiles, dtype=jnp.int32)
    slot_of = slots + jnp.sum(
        jnp.where(names[None, :] == places[:, None], number[None, :] - slots, 0), axis=1
    )
    half = users_share // 2
    users = jnp.concatenate([user_factors[:half], user_factors[half:]], axis=1)
    items = jnp.concatenate([item_factors, item_factors], axis=1)

    bf16, f32 = jnp.bfloat16, jnp.float32
    dma = pltpu.SemaphoreType.DMA

    def gather_sems(size):
        return [dma((size // 2,))] * 4

    def scatter_scratch(size, share):
        outer = size // 2
        return [
            pltpu.VMEM((outer, share, vecs), f32),
            pltpu.VMEM((outer, share, vecs), bf16),
            pltpu.VMEM((outer, share, vecs), bf16),
            pltpu.VMEM((outer, share, vecs), bf16),
            pltpu.VMEM((outer, share, vecs), bf16),
        ] + gather_sems(size)

    scratch = [
        pltpu.VMEM((n_col, half, 2 * rank), bf16),
        pltpu.VMEM((n_row, items_share, 2 * rank), bf16),
        pltpu.VMEM((n_row, items_share, vecs), bf16),
        pltpu.VMEM((user_tiles, tile, 2 * rank), bf16),
        pltpu.VMEM((item_tiles, tile, 2 * rank), bf16),
        pltpu.VMEM((slots + 1, tile, tile), bf16),
        pltpu.VMEM((slots + 1, tile, tile), bf16),
        pltpu.VMEM((users_block, items_block), bf16),
        pltpu.VMEM((items_block, users_block), bf16),
        pltpu.VMEM((vecs, vecs), f32),
    ]
    scratch += gather_sems(n_col) + gather_sems(n_row) + gather_sems(n_row)
    for _ in range(ITERS):
        scratch += scatter_scratch(n_col, users_share)
        scratch += scatter_scratch(n_row, items_share)
        scratch += [pltpu.VMEM((n_col, users_share, vecs), bf16)] + gather_sems(n_col)
    for _ in range(ITERS - 1):
        scratch += [pltpu.VMEM((n_row, items_share, vecs), bf16)] + gather_sems(n_row)
    for _ in range(2 * ITERS):
        part = vecs // n_col
        scratch += [
            pltpu.VMEM((n_col, part, vecs), f32),
            pltpu.VMEM((n_col, part, vecs), f32),
            pltpu.VMEM((1, part, vecs), f32),
            pltpu.VMEM((n_row, part, vecs), f32),
            pltpu.VMEM((n_col, part, vecs), f32),
        ]
        scratch += [dma((n_col,)), dma((n_col,)), dma((n_row,)), dma((n_row,)), dma((n_col,)), dma((n_col,))]

    smem, vmem = pl.BlockSpec(memory_space=pltpu.SMEM), pl.BlockSpec(memory_space=pltpu.VMEM)
    user_basis, item_basis = pl.pallas_call(
        functools.partial(kernel, n_row, n_col),
        out_shape=(
            jax.ShapeDtypeStruct((users_share, vecs), f32),
            jax.ShapeDtypeStruct((items_share, vecs), f32),
        ),
        in_specs=[smem] * 3 + [vmem] * 4,
        out_specs=(vmem, vmem),
        scratch_shapes=scratch,
        compiler_params=pltpu.CompilerParams(
            collective_id=0, has_side_effects=True, vmem_limit_bytes=62 * 1024 * 1024
        ),
    )(rows, cols, slot_of, users, items, start_vectors, ratings[0, 0])
    users_total = users_share * n_row * n_col
    items_total = items_share * n_row * n_col
    return (
        user_basis * jnp.sqrt(jnp.float32(users_total)),
        item_basis * jnp.sqrt(jnp.float32(items_total)),
    )


def solution(mesh):
    in_specs = (
        P(("row", "col"), None),
        P(("col", "row"), None),
        P(("col", "row"), None),
        P("row", "col", None, None, None),
        P("row", "col", None),
        P("row", "col", None),
        P("row", "col"),
    )
    out_specs = (P(("row", "col"), None), P(("col", "row"), None))
    body = functools.partial(shards, mesh.shape["row"], mesh.shape["col"])
    return jax.shard_map(body, mesh=mesh, in_specs=in_specs, out_specs=out_specs, check_vma=False)
```

```python
import functools

import jax
import jax.numpy as jnp
from jax import lax
from jax.experimental import pallas as pl
from jax.experimental.pallas import tpu as pltpu
from jax.sharding import PartitionSpec as P

MESH = pl.DeviceIdType.MESH
HIGHEST = lax.Precision.HIGHEST
ITERS = 2
UNROLL = 4
PANEL = 32
SUB = 8


def aligned(index, size):
    return pl.ds(pl.multiple_of(index * size, size), size)


class Group:
    def __init__(self, axis, size, other_axis):
        self.axis = axis
        self.size = size
        self.outer = size // 2
        self.me = lax.axis_index(axis)
        self.other = lax.axis_index(other_axis)
        self.o = self.me // 2
        self.i = self.me % 2

    def device(self, index):
        if self.axis == "col":
            return (self.other, index)
        return (index, self.other)

    def ahead(self, t):
        return (self.o + t) % self.outer

    def behind(self, t):
        return (self.o + self.outer - t) % self.outer


def remote(src, dst, send, recv, device):
    return pltpu.make_async_remote_copy(
        src_ref=src, dst_ref=dst, send_sem=send, recv_sem=recv, device_id=device, device_id_type=MESH
    )


class Gather:
    def __init__(self, group, full, sems):
        self.group, self.full = group, full
        self.outer_send, self.outer_recv, self.inner_send, self.inner_recv = sems

    def outer_copy(self, t):
        g = self.group
        block = self.full.at[g.me]
        return remote(
            block, block, self.outer_send.at[t], self.outer_recv.at[t], g.device(g.ahead(t) * 2 + g.i)
        )

    def outer_arrival(self, t):
        g = self.group
        block = self.full.at[g.behind(t) * 2 + g.i]
        return remote(
            block, block, self.outer_send.at[t], self.outer_recv.at[t], g.device(g.ahead(t) * 2 + g.i)
        )

    def inner_copy(self, t):
        g = self.group
        block = self.full.at[g.behind(t) * 2 + g.i]
        return remote(
            block, block, self.inner_send.at[t], self.inner_recv.at[t], g.device(g.o * 2 + 1 - g.i)
        )

    def inner_arrival(self, t):
        g = self.group
        block = self.full.at[g.behind(t) * 2 + 1 - g.i]
        return remote(
            block, block, self.inner_send.at[t], self.inner_recv.at[t], g.device(g.o * 2 + 1 - g.i)
        )

    def start(self):
        for t in range(self.group.outer - 1, 0, -1):
            self.outer_copy(t).start()
        self.inner_copy(0).start()

    def forward(self, t):
        self.outer_arrival(t).wait_recv()
        self.inner_copy(t).start()

    def finish(self):
        for t in range(1, self.group.outer):
            self.forward(t)
        self.arrivals()

    def arrivals(self):
        for t in range(self.group.outer):
            self.inner_arrival(t).wait_recv()

    def drain(self):
        for t in range(1, self.group.outer):
            self.outer_copy(t).wait_send()
        for t in range(self.group.outer):
            self.inner_copy(t).wait_send()


class Scatter:
    def __init__(self, group, own, inner_out, inner_in, outer_out, outer_in, sems):
        self.group = group
        self.own, self.inner_out, self.inner_in = own, inner_out, inner_in
        self.outer_out, self.outer_in = outer_out, outer_in
        self.outer_send, self.outer_recv, self.inner_send, self.inner_recv = sems

    def inner_copy(self, t):
        g = self.group
        return remote(
            self.inner_out.at[t],
            self.inner_in.at[t],
            self.inner_send.at[t],
            self.inner_recv.at[t],
            g.device(g.o * 2 + 1 - g.i),
        )

    def outer_copy(self, t):
        g = self.group
        return remote(
            self.outer_out.at[t],
            self.outer_in.at[t],
            self.outer_send.at[t],
            self.outer_recv.at[t],
            g.device(g.ahead(t) * 2 + g.i),
        )

    def products(self, matrix, basis):
        g = self.group
        share = self.own.shape[1]
        chunk = min(share, 512)

        def block(index, store):
            def part(h, _):
                base = pl.multiple_of(index * share + h * chunk, chunk)
                store(
                    h,
                    jnp.dot(
                        matrix[pl.ds(base, chunk), :], basis(), preferred_element_type=jnp.float32
                    ),
                )
                return 0

            lax.fori_loop(0, share // chunk, part, 0)

        def step(s, _):
            t = (s + 1) % g.outer
            there = g.ahead(t)

            def store_out(h, value):
                self.inner_out[t, aligned(h, chunk), :] = value.astype(jnp.bfloat16)

            def store_own(h, value):
                self.own[t, aligned(h, chunk), :] = value

            block(there * 2 + 1 - g.i, store_out)
            self.inner_copy(t).start()
            block(there * 2 + g.i, store_own)
            return 0

        lax.fori_loop(0, g.outer, step, 0)

    def pass_on(self, beside=()):
        beside = list(beside)

        def step(t):
            self.inner_copy(t).wait_recv()
            self.outer_out[t] = (self.own[t] + self.inner_in[t].astype(jnp.float32)).astype(
                jnp.bfloat16
            )
            self.outer_copy(t).start()

        for t in range(1, self.group.outer):
            step(t)
            if beside:
                beside.pop(0)()
        for part in beside:
            part()

    def total(self):
        self.inner_copy(0).wait_recv()
        self.own[0] = self.own[0] + self.inner_in[0].astype(jnp.float32)

        def step(t, _):
            self.outer_copy(t).wait_recv()
            self.own[0] = self.own[0] + self.outer_in[t].astype(jnp.float32)
            return 0

        lax.fori_loop(1, self.group.outer, step, 0)

    def drain(self):
        for t in range(1, self.group.outer):
            self.outer_copy(t).wait_send()
        for t in range(self.group.outer):
            self.inner_copy(t).wait_send()


class Gram:
    def __init__(self, row, col, parts, arrived, mine, others, full, sems):
        self.row, self.col = row, col
        self.parts, self.arrived, self.mine, self.others, self.full = parts, arrived, mine, others, full
        self.sems = sems

    def scatter_copy(self, t):
        c = self.col
        there = (c.me + t) % c.size
        return remote(
            self.parts.at[there],
            self.arrived.at[t],
            self.sems[0].at[t],
            self.sems[1].at[t],
            c.device(there),
        )

    def exchange_copy(self, t):
        r = self.row
        return remote(
            self.mine.at[0],
            self.others.at[t],
            self.sems[2].at[t],
            self.sems[3].at[t],
            r.device((r.me + t) % r.size),
        )

    def gather_copy(self, t):
        c = self.col
        return remote(
            self.full.at[c.me],
            self.full.at[c.me],
            self.sems[4].at[t],
            self.sems[5].at[t],
            c.device((c.me + t) % c.size),
        )

    def gather_arrival(self, t):
        c = self.col
        block = self.full.at[(c.me + c.size - t) % c.size]
        return remote(
            block, block, self.sems[4].at[t], self.sems[5].at[t], c.device((c.me + t) % c.size)
        )

    def begin(self, block):
        gram = lax.dot_general(
            block, block, (((0,), (0,)), ((), ())), precision=HIGHEST, preferred_element_type=jnp.float32
        )
        rows = self.parts.shape[1]
        for index in range(self.col.size):
            self.parts[index] = gram[index * rows : (index + 1) * rows, :]
        for t in range(1, self.col.size):
            self.scatter_copy(t).start()

    def exchange(self):
        for t in range(1, self.col.size):
            self.scatter_copy(t).wait_recv()
        total = self.parts[self.col.me]
        for t in range(1, self.col.size):
            total = total + self.arrived[t]
        self.mine[0] = total
        for t in range(1, self.row.size):
            self.exchange_copy(t).start()

    def spread(self):
        for t in range(1, self.row.size):
            self.exchange_copy(t).wait_recv()
        total = self.mine[0]
        for t in range(1, self.row.size):
            total = total + self.others[t]
        self.full[self.col.me] = total
        for t in range(1, self.col.size):
            self.gather_copy(t).start()

    def collect(self, work):
        for t in range(1, self.col.size):
            self.gather_arrival(t).wait_recv()
        rows = self.parts.shape[1]
        for index in range(self.col.size):
            work[index * rows : (index + 1) * rows, :] = self.full[index]

    def drain(self):
        for t in range(1, self.col.size):
            self.scatter_copy(t).wait_send()
            self.gather_copy(t).wait_send()
        for t in range(1, self.row.size):
            self.exchange_copy(t).wait_send()


def eliminate(work, panel):
    size = work.shape[0]
    base = panel * PANEL if isinstance(panel, int) else pl.multiple_of(panel * PANEL, PANEL)
    lanes = lax.broadcasted_iota(jnp.int32, (PANEL, size), 1)
    subs = lax.broadcasted_iota(jnp.int32, (PANEL, size), 0)
    done, active = [], work[pl.ds(base, PANEL), :]
    for q in range(PANEL // SUB):
        lane, sub = lanes[q * SUB :], subs[: PANEL - q * SUB]
        columns = []
        for b in range(SUB):
            picked = jnp.where(lane == base + q * SUB + b, active, 0.0)
            columns.append(jnp.broadcast_to(jnp.sum(picked, axis=1, keepdims=True), active.shape))
        for a in range(SUB):
            here = lane == base + q * SUB + a
            inverse = 1.0 / columns[a][a : a + 1, :]
            factor = jnp.where(sub > a, columns[a] * inverse, 0.0)
            row = jnp.where(here[:1], 1.0, active[a : a + 1, :])
            active = jnp.where(here & (sub > a), 0.0, active) - factor * row
            for b in range(a + 1, SUB):
                columns[b] = columns[b] - factor * columns[b][a : a + 1, :]
        done.append(active[:SUB])
        active = active[SUB:]
    rows = jnp.concatenate(done, axis=0)
    work[pl.ds(base, PANEL), :] = rows
    diagonal = lanes == base + subs
    pivots = jnp.sum(jnp.where(diagonal, rows, 0.0), axis=1, keepdims=True)
    inside = (lanes >= base) & (lanes < base + PANEL)
    factors = jnp.where(lanes >= base + PANEL, rows, 0.0) / pivots
    full = jnp.where(inside & (lanes > base + subs), 0.0, jnp.where(diagonal, 1.0, rows))
    update = lax.dot_general(
        factors, full, (((0,), (0,)), ((), ())), precision=HIGHEST, preferred_element_type=jnp.float32
    )
    lane = lax.broadcasted_iota(jnp.int32, (size, size), 1)
    sub = lax.broadcasted_iota(jnp.int32, (size, size), 0)
    fresh = (lane >= base) & (lane < base + PANEL) & (sub >= base + PANEL)
    work[...] = jnp.where(fresh, 0.0, work[...]) - update


def inverse_factor(work):
    size = work.shape[0]
    lanes = lax.broadcasted_iota(jnp.int32, (size, size), 1)
    subs = lax.broadcasted_iota(jnp.int32, (size, size), 0)
    matrix = work[...]
    pivots = jnp.sum(jnp.where(lanes == subs, matrix, 0.0), axis=1, keepdims=True)
    unit = jnp.where(lanes == subs, 1.0, jnp.where(lanes < subs, matrix, 0.0))
    return unit * lax.rsqrt(pivots)


def times_transposed(block, inverse):
    return lax.dot_general(
        block, inverse, (((1,), (1,)), ((), ())), precision=HIGHEST, preferred_element_type=jnp.float32
    )


def kernel(n_row, n_col, *refs):
    refs = list(refs)

    def take(count):
        got = refs[:count]
        del refs[:count]
        return got

    rows, cols, slot_of, users, items, start, ratings = take(7)
    user_out, item_out = take(2)
    user_full, item_full, start_full, user_wide, item_wide, res, res_t, block, block_t, work = take(10)
    row = Group("row", n_row, "col")
    col = Group("col", n_col, "row")
    user_gather = Gather(col, user_full, take(4))
    item_gather = Gather(row, item_full, take(4))
    start_gather = Gather(row, start_full, take(4))
    forward_sums, backward_sums, user_gathers, item_gathers, grams = [], [], [], [], []
    for _ in range(ITERS):
        forward_sums.append(Scatter(col, *take(5), take(4)))
        backward_sums.append(Scatter(row, *take(5), take(4)))
        user_gathers.append(Gather(col, *take(1), take(4)))
    for _ in range(ITERS - 1):
        item_gathers.append(Gather(row, *take(1), take(4)))
    for _ in range(2 * ITERS):
        grams.append(Gram(row, col, *take(5), take(6)))
    assert not refs

    barrier = pltpu.get_barrier_semaphore()
    for group in (row, col):
        for t in range(1, group.size):
            pl.semaphore_signal(
                barrier, inc=1, device_id=group.device((group.me + t) % group.size), device_id_type=MESH
            )
    pl.semaphore_wait(barrier, n_row + n_col - 2)

    user_full[col.me] = users[...]
    user_gather.start()
    item_full[row.me] = items[...]
    item_gather.start()
    start_full[row.me] = start[...]
    start_gather.start()

    slots, tile, _ = ratings.shape
    user_tiles = block.shape[0] // tile
    item_tiles = block.shape[1] // tile
    res[slots] = jnp.zeros((tile, tile), jnp.bfloat16)

    item_gather.finish()
    user_gather.finish()

    half = users.shape[0]
    rank = users.shape[1] // 2
    piece = min(half, tile)
    low = lax.broadcasted_iota(jnp.int32, (piece, 2 * rank), 1) < rank

    def widen(index, _):
        for side in range(2):
            for base in range(0, half, piece):
                packed = user_full[index, base : base + piece, :].astype(jnp.float32)
                value = jnp.where(low, packed, 0.0) if side == 0 else jnp.where(low, 0.0, packed)
                place = index * 2 * half + side * half + base
                inside = pl.ds(pl.multiple_of(place % tile, piece), piece)
                user_wide[place // tile, inside, :] = value.astype(jnp.bfloat16)
        return 0

    lax.fori_loop(0, n_col, widen, 0)
    per_share = item_full.shape[1] // tile
    for index in range(n_row):
        for q in range(per_share):
            item_wide[index * per_share + q] = item_full[index, q * tile : (q + 1) * tile, :]

    def residual(s, _):
        for u in range(UNROLL):
            k = s * UNROLL + u
            left = user_wide[rows[k]]
            right = item_wide[cols[k]]
            product = lax.dot_general(
                left, right, (((1,), (1,)), ((), ())), preferred_element_type=jnp.float32
            )
            value = product - ratings[k].astype(jnp.float32)
            res[k] = value.astype(jnp.bfloat16)
        return 0

    lax.fori_loop(0, slots // UNROLL, residual, 0)

    def lay_row(a, _):
        for b in range(item_tiles):
            block[aligned(a, tile), b * tile : (b + 1) * tile] = res[slot_of[a * item_tiles + b]]
        return 0

    lax.fori_loop(0, user_tiles, lay_row, 0)

    def transposes():
        def some(s, _):
            for u in range(UNROLL):
                res_t[s * UNROLL + u] = res[s * UNROLL + u].T
            return 0

        res_t[slots] = jnp.zeros((tile, tile), jnp.bfloat16)
        lax.fori_loop(0, slots // UNROLL, some, 0)

    def lay_columns(first, end):
        def lay(b, _):
            for a in range(user_tiles):
                block_t[aligned(b, tile), a * tile : (a + 1) * tile] = res_t[
                    slot_of[a * item_tiles + b]
                ]
            return 0

        lax.fori_loop(first, end, lay, 0)

    start_gather.finish()

    panels = work.shape[0] // PANEL

    def eliminate_from(first):
        def panel(index, _):
            eliminate(work, index)
            return 0

        lax.fori_loop(first, panels, panel, 0)

    def whole(full):
        return lambda: full[...].reshape(full.shape[0] * full.shape[1], full.shape[2])

    def apply(sums):
        return times_transposed(sums.own[0], inverse_factor(work))

    items_now = start_full
    for index in range(ITERS):
        last = index == ITERS - 1
        sums, gram, gather = forward_sums[index], grams[2 * index], user_gathers[index]
        sums.products(block, whole(items_now))
        if index == 0:
            middle = item_tiles // 2
            sums.pass_on(
                [
                    transposes,
                    lambda: lay_columns(0, middle),
                    lambda: lay_columns(middle, item_tiles),
                ]
            )
            sums.total()
        else:
            grams[2 * index - 1].collect(work)
            sums.pass_on([functools.partial(eliminate, work, panel) for panel in range(panels)])
            sums.total()
            sums.own[0] = apply(sums)
        gather.full[col.me] = sums.own[0].astype(jnp.bfloat16)
        gather.start()
        gram.begin(sums.own[0])
        gram.exchange()
        gather.forward(1)
        gram.spread()
        for t in range(2, col.outer):
            gather.forward(t)
        gram.collect(work)
        eliminate_from(0)
        if last:
            user_out[...] = apply(sums)
        gather.arrivals()
        sums, gram = backward_sums[index], grams[2 * index + 1]
        sums.products(block_t, whole(gather.full))
        sums.pass_on()
        sums.total()
        sums.own[0] = apply(sums)
        if not last:
            gather = item_gathers[index]
            gather.full[row.me] = sums.own[0].astype(jnp.bfloat16)
            gather.start()
            gram.begin(sums.own[0])
            gather.finish()
            gram.exchange()
            gram.spread()
            items_now = gather.full
        else:
            gram.begin(sums.own[0])
            gram.exchange()
            gram.spread()
            gram.collect(work)
            eliminate_from(0)
            item_out[...] = apply(sums)

    for part in (
        [user_gather, item_gather, start_gather]
        + forward_sums
        + backward_sums
        + user_gathers
        + item_gathers
        + grams
    ):
        part.drain()


def shards(n_row, n_col, user_factors, item_factors, start_vectors, ratings, tile_rows, tile_cols, tile_count):
    slots, tile = ratings.shape[2], ratings.shape[-1]
    vecs = start_vectors.shape[1]
    users_share, rank = user_factors.shape
    items_share = item_factors.shape[0]
    users_block, items_block = users_share * n_col, items_share * n_row
    user_tiles, item_tiles = users_block // tile, items_block // tile
    rows, cols = tile_rows[0, 0], tile_cols[0, 0]
    number = jnp.arange(slots, dtype=jnp.int32)
    names = jnp.where(number < tile_count[0, 0], rows * item_tiles + cols, -1)
    places = jnp.arange(user_tiles * item_tiles, dtype=jnp.int32)
    slot_of = slots + jnp.sum(
        jnp.where(names[None, :] == places[:, None], number[None, :] - slots, 0), axis=1
    )
    half = users_share // 2
    users = jnp.concatenate([user_factors[:half], user_factors[half:]], axis=1)
    items = jnp.concatenate([item_factors, item_factors], axis=1)

    bf16, f32 = jnp.bfloat16, jnp.float32
    dma = pltpu.SemaphoreType.DMA

    def gather_sems(size):
        return [dma((size // 2,))] * 4

    def scatter_scratch(size, share):
        outer = size // 2
        return [
            pltpu.VMEM((outer, share, vecs), f32),
            pltpu.VMEM((outer, share, vecs), bf16),
            pltpu.VMEM((outer, share, vecs), bf16),
            pltpu.VMEM((outer, share, vecs), bf16),
            pltpu.VMEM((outer, share, vecs), bf16),
        ] + gather_sems(size)

    scratch = [
        pltpu.VMEM((n_col, half, 2 * rank), bf16),
        pltpu.VMEM((n_row, items_share, 2 * rank), bf16),
        pltpu.VMEM((n_row, items_share, vecs), bf16),
        pltpu.VMEM((user_tiles, tile, 2 * rank), bf16),
        pltpu.VMEM((item_tiles, tile, 2 * rank), bf16),
        pltpu.VMEM((slots + 1, tile, tile), bf16),
        pltpu.VMEM((slots + 1, tile, tile), bf16),
        pltpu.VMEM((users_block, items_block), bf16),
        pltpu.VMEM((items_block, users_block), bf16),
        pltpu.VMEM((vecs, vecs), f32),
    ]
    scratch += gather_sems(n_col) + gather_sems(n_row) + gather_sems(n_row)
    for _ in range(ITERS):
        scratch += scatter_scratch(n_col, users_share)
        scratch += scatter_scratch(n_row, items_share)
        scratch += [pltpu.VMEM((n_col, users_share, vecs), bf16)] + gather_sems(n_col)
    for _ in range(ITERS - 1):
        scratch += [pltpu.VMEM((n_row, items_share, vecs), bf16)] + gather_sems(n_row)
    for _ in range(2 * ITERS):
        part = vecs // n_col
        scratch += [
            pltpu.VMEM((n_col, part, vecs), f32),
            pltpu.VMEM((n_col, part, vecs), f32),
            pltpu.VMEM((1, part, vecs), f32),
            pltpu.VMEM((n_row, part, vecs), f32),
            pltpu.VMEM((n_col, part, vecs), f32),
        ]
        scratch += [dma((n_col,)), dma((n_col,)), dma((n_row,)), dma((n_row,)), dma((n_col,)), dma((n_col,))]

    smem, vmem = pl.BlockSpec(memory_space=pltpu.SMEM), pl.BlockSpec(memory_space=pltpu.VMEM)
    user_basis, item_basis = pl.pallas_call(
        functools.partial(kernel, n_row, n_col),
        out_shape=(
            jax.ShapeDtypeStruct((users_share, vecs), f32),
            jax.ShapeDtypeStruct((items_share, vecs), f32),
        ),
        in_specs=[smem] * 3 + [vmem] * 4,
        out_specs=(vmem, vmem),
        scratch_shapes=scratch,
        compiler_params=pltpu.CompilerParams(
            collective_id=0, has_side_effects=True, vmem_limit_bytes=62 * 1024 * 1024
        ),
    )(rows, cols, slot_of, users, items, start_vectors, ratings[0, 0])
    users_total = users_share * n_row * n_col
    items_total = items_share * n_row * n_col
    return (
        user_basis * jnp.sqrt(jnp.float32(users_total)),
        item_basis * jnp.sqrt(jnp.float32(items_total)),
    )


def solution(mesh):
    in_specs = (
        P(("row", "col"), None),
        P(("col", "row"), None),
        P(("col", "row"), None),
        P("row", "col", None, None, None),
        P("row", "col", None),
        P("row", "col", None),
        P("row", "col"),
    )
    out_specs = (P(("row", "col"), None), P(("col", "row"), None))
    body = functools.partial(shards, mesh.shape["row"], mesh.shape["col"])
    return jax.shard_map(body, mesh=mesh, in_specs=in_specs, out_specs=out_specs, check_vma=False)
```

```python
import functools

import jax
import jax.numpy as jnp
from jax import lax
from jax.experimental import pallas as pl
from jax.experimental.pallas import tpu as pltpu
from jax.sharding import PartitionSpec as P

MESH = pl.DeviceIdType.MESH
HIGHEST = lax.Precision.HIGHEST
ITERS = 2
UNROLL = 4
TILE = 128
PANEL = 32
SUB = 8


def aligned(index, size):
    return pl.ds(pl.multiple_of(index * size, size), size)


class Group:
    def __init__(self, axis, size, other_axis):
        self.axis = axis
        self.size = size
        self.outer = size // 2
        self.me = lax.axis_index(axis)
        self.other = lax.axis_index(other_axis)
        self.o = self.me // 2
        self.i = self.me % 2

    def device(self, index):
        if self.axis == "col":
            return (self.other, index)
        return (index, self.other)

    def ahead(self, t):
        return (self.o + t) % self.outer

    def behind(self, t):
        return (self.o + self.outer - t) % self.outer


def remote(src, dst, send, recv, device):
    return pltpu.make_async_remote_copy(
        src_ref=src, dst_ref=dst, send_sem=send, recv_sem=recv, device_id=device, device_id_type=MESH
    )


class Gather:
    def __init__(self, group, full, sems):
        self.group, self.full = group, full
        self.outer_send, self.outer_recv, self.inner_send, self.inner_recv = sems

    def outer_copy(self, t):
        g = self.group
        block = self.full.at[g.me]
        return remote(
            block, block, self.outer_send.at[t], self.outer_recv.at[t], g.device(g.ahead(t) * 2 + g.i)
        )

    def outer_arrival(self, t):
        g = self.group
        block = self.full.at[g.behind(t) * 2 + g.i]
        return remote(
            block, block, self.outer_send.at[t], self.outer_recv.at[t], g.device(g.ahead(t) * 2 + g.i)
        )

    def inner_copy(self, t):
        g = self.group
        block = self.full.at[g.behind(t) * 2 + g.i]
        return remote(
            block, block, self.inner_send.at[t], self.inner_recv.at[t], g.device(g.o * 2 + 1 - g.i)
        )

    def inner_arrival(self, t):
        g = self.group
        block = self.full.at[g.behind(t) * 2 + 1 - g.i]
        return remote(
            block, block, self.inner_send.at[t], self.inner_recv.at[t], g.device(g.o * 2 + 1 - g.i)
        )

    def start(self):
        for t in range(self.group.outer - 1, 0, -1):
            self.outer_copy(t).start()
        self.inner_copy(0).start()

    def forward(self, t):
        self.outer_arrival(t).wait_recv()
        self.inner_copy(t).start()

    def finish(self):
        for t in range(1, self.group.outer):
            self.forward(t)
        self.arrivals()

    def arrivals(self):
        for t in range(self.group.outer):
            self.inner_arrival(t).wait_recv()

    def drain(self):
        for t in range(1, self.group.outer):
            self.outer_copy(t).wait_send()
        for t in range(self.group.outer):
            self.inner_copy(t).wait_send()


class Scatter:
    def __init__(self, group, own, inner_out, inner_in, outer_out, outer_in, sems):
        self.group = group
        self.own, self.inner_out, self.inner_in = own, inner_out, inner_in
        self.outer_out, self.outer_in = outer_out, outer_in
        self.outer_send, self.outer_recv, self.inner_send, self.inner_recv = sems

    def inner_copy(self, t):
        g = self.group
        return remote(
            self.inner_out.at[t],
            self.inner_in.at[t],
            self.inner_send.at[t],
            self.inner_recv.at[t],
            g.device(g.o * 2 + 1 - g.i),
        )

    def outer_copy(self, t):
        g = self.group
        return remote(
            self.outer_out.at[t],
            self.outer_in.at[t],
            self.outer_send.at[t],
            self.outer_recv.at[t],
            g.device(g.ahead(t) * 2 + g.i),
        )

    def send_products(self, fetch):
        g = self.group
        share = self.own.shape[1]
        per = share // TILE

        def step(s, _):
            t = (s + 1) % g.outer
            there = g.ahead(t)
            for q in range(per):
                place = pl.ds(q * TILE, TILE)
                tile = fetch((there * 2 + 1 - g.i) * per + q)
                self.inner_out[t, place, :] = tile.astype(jnp.bfloat16)
            self.inner_copy(t).start()
            for q in range(per):
                self.own[t, pl.ds(q * TILE, TILE), :] = fetch((there * 2 + g.i) * per + q)
            return 0

        lax.fori_loop(0, g.outer, step, 0)

    def pass_on(self, beside=()):
        beside = list(beside)

        def step(t):
            self.inner_copy(t).wait_recv()
            self.outer_out[t] = (self.own[t] + self.inner_in[t].astype(jnp.float32)).astype(
                jnp.bfloat16
            )
            self.outer_copy(t).start()

        for t in range(1, self.group.outer):
            step(t)
            if beside:
                beside.pop(0)()
        for part in beside:
            part()

    def total(self):
        self.inner_copy(0).wait_recv()
        self.own[0] = self.own[0] + self.inner_in[0].astype(jnp.float32)

        def step(t, _):
            self.outer_copy(t).wait_recv()
            self.own[0] = self.own[0] + self.outer_in[t].astype(jnp.float32)
            return 0

        lax.fori_loop(1, self.group.outer, step, 0)

    def drain(self):
        for t in range(1, self.group.outer):
            self.outer_copy(t).wait_send()
        for t in range(self.group.outer):
            self.inner_copy(t).wait_send()


class Gram:
    def __init__(self, row, col, parts, arrived, mine, others, full, sems):
        self.row, self.col = row, col
        self.parts, self.arrived, self.mine, self.others, self.full = parts, arrived, mine, others, full
        self.sems = sems

    def scatter_copy(self, t):
        c = self.col
        there = (c.me + t) % c.size
        return remote(
            self.parts.at[there],
            self.arrived.at[t],
            self.sems[0].at[t],
            self.sems[1].at[t],
            c.device(there),
        )

    def exchange_copy(self, t):
        r = self.row
        return remote(
            self.mine.at[0],
            self.others.at[t],
            self.sems[2].at[t],
            self.sems[3].at[t],
            r.device((r.me + t) % r.size),
        )

    def gather_copy(self, t):
        c = self.col
        return remote(
            self.full.at[c.me],
            self.full.at[c.me],
            self.sems[4].at[t],
            self.sems[5].at[t],
            c.device((c.me + t) % c.size),
        )

    def gather_arrival(self, t):
        c = self.col
        block = self.full.at[(c.me + c.size - t) % c.size]
        return remote(
            block, block, self.sems[4].at[t], self.sems[5].at[t], c.device((c.me + t) % c.size)
        )

    def begin(self, block):
        gram = lax.dot_general(
            block, block, (((0,), (0,)), ((), ())), precision=HIGHEST, preferred_element_type=jnp.float32
        )
        rows = self.parts.shape[1]
        for index in range(self.col.size):
            self.parts[index] = gram[index * rows : (index + 1) * rows, :]
        for t in range(1, self.col.size):
            self.scatter_copy(t).start()

    def exchange(self):
        for t in range(1, self.col.size):
            self.scatter_copy(t).wait_recv()
        total = self.parts[self.col.me]
        for t in range(1, self.col.size):
            total = total + self.arrived[t]
        self.mine[0] = total
        for t in range(1, self.row.size):
            self.exchange_copy(t).start()

    def spread(self):
        for t in range(1, self.row.size):
            self.exchange_copy(t).wait_recv()
        total = self.mine[0]
        for t in range(1, self.row.size):
            total = total + self.others[t]
        self.full[self.col.me] = total
        for t in range(1, self.col.size):
            self.gather_copy(t).start()

    def collect(self, work):
        for t in range(1, self.col.size):
            self.gather_arrival(t).wait_recv()
        rows = self.parts.shape[1]
        for index in range(self.col.size):
            work[index * rows : (index + 1) * rows, :] = self.full[index]

    def drain(self):
        for t in range(1, self.col.size):
            self.scatter_copy(t).wait_send()
            self.gather_copy(t).wait_send()
        for t in range(1, self.row.size):
            self.exchange_copy(t).wait_send()


def eliminate(work, panel):
    size = work.shape[0]
    base = panel * PANEL if isinstance(panel, int) else pl.multiple_of(panel * PANEL, PANEL)
    lanes = lax.broadcasted_iota(jnp.int32, (PANEL, size), 1)
    subs = lax.broadcasted_iota(jnp.int32, (PANEL, size), 0)
    done, active = [], work[pl.ds(base, PANEL), :]
    for q in range(PANEL // SUB):
        lane, sub = lanes[q * SUB :], subs[: PANEL - q * SUB]
        columns = []
        for b in range(SUB):
            picked = jnp.where(lane == base + q * SUB + b, active, 0.0)
            columns.append(jnp.broadcast_to(jnp.sum(picked, axis=1, keepdims=True), active.shape))
        for a in range(SUB):
            here = lane == base + q * SUB + a
            inverse = 1.0 / columns[a][a : a + 1, :]
            factor = jnp.where(sub > a, columns[a] * inverse, 0.0)
            row = jnp.where(here[:1], 1.0, active[a : a + 1, :])
            active = jnp.where(here & (sub > a), 0.0, active) - factor * row
            for b in range(a + 1, SUB):
                columns[b] = columns[b] - factor * columns[b][a : a + 1, :]
        done.append(active[:SUB])
        active = active[SUB:]
    rows = jnp.concatenate(done, axis=0)
    work[pl.ds(base, PANEL), :] = rows
    diagonal = lanes == base + subs
    pivots = jnp.sum(jnp.where(diagonal, rows, 0.0), axis=1, keepdims=True)
    inside = (lanes >= base) & (lanes < base + PANEL)
    factors = jnp.where(lanes >= base + PANEL, rows, 0.0) / pivots
    full = jnp.where(inside & (lanes > base + subs), 0.0, jnp.where(diagonal, 1.0, rows))
    update = lax.dot_general(
        factors, full, (((0,), (0,)), ((), ())), precision=HIGHEST, preferred_element_type=jnp.float32
    )
    lane = lax.broadcasted_iota(jnp.int32, (size, size), 1)
    sub = lax.broadcasted_iota(jnp.int32, (size, size), 0)
    fresh = (lane >= base) & (lane < base + PANEL) & (sub >= base + PANEL)
    work[...] = jnp.where(fresh, 0.0, work[...]) - update


def inverse_factor(work):
    size = work.shape[0]
    lanes = lax.broadcasted_iota(jnp.int32, (size, size), 1)
    subs = lax.broadcasted_iota(jnp.int32, (size, size), 0)
    matrix = work[...]
    pivots = jnp.sum(jnp.where(lanes == subs, matrix, 0.0), axis=1, keepdims=True)
    unit = jnp.where(lanes == subs, 1.0, jnp.where(lanes < subs, matrix, 0.0))
    return unit * lax.rsqrt(pivots)


def times_transposed(block, inverse):
    return lax.dot_general(
        block, inverse, (((1,), (1,)), ((), ())), precision=HIGHEST, preferred_element_type=jnp.float32
    )


def kernel(n_row, n_col, *refs):
    refs = list(refs)

    def take(count):
        got = refs[:count]
        del refs[:count]
        return got

    slot_of, row_of, col_of, from_slot, back_row, keep, user_last, item_last = take(8)
    users, items, start, ratings = take(4)
    user_out, item_out = take(2)
    user_full, item_full, start_full, user_wide, item_wide, res, res_t, basis_tiles, sums_of, work = take(10)
    row = Group("row", n_row, "col")
    col = Group("col", n_col, "row")
    user_gather = Gather(col, user_full, take(4))
    item_gather = Gather(row, item_full, take(4))
    start_gather = Gather(row, start_full, take(4))
    forward_sums, backward_sums, user_gathers, item_gathers, grams = [], [], [], [], []
    for _ in range(ITERS):
        forward_sums.append(Scatter(col, *take(5), take(4)))
        backward_sums.append(Scatter(row, *take(5), take(4)))
        user_gathers.append(Gather(col, *take(1), take(4)))
    for _ in range(ITERS - 1):
        item_gathers.append(Gather(row, *take(1), take(4)))
    for _ in range(2 * ITERS):
        grams.append(Gram(row, col, *take(5), take(6)))
    assert not refs

    barrier = pltpu.get_barrier_semaphore()
    for group in (row, col):
        for t in range(1, group.size):
            pl.semaphore_signal(
                barrier, inc=1, device_id=group.device((group.me + t) % group.size), device_id_type=MESH
            )
    pl.semaphore_wait(barrier, n_row + n_col - 2)

    user_full[col.me] = users[...]
    user_gather.start()
    item_full[row.me] = items[...]
    item_gather.start()
    start_full[row.me] = start[...]
    start_gather.start()

    slots, tile, _ = ratings.shape
    sums_of[slots] = jnp.zeros(sums_of.shape[1:], jnp.float32)

    item_gather.finish()
    user_gather.finish()

    half = users.shape[0]
    rank = users.shape[1] // 2
    piece = min(half, tile)
    low = lax.broadcasted_iota(jnp.int32, (piece, 2 * rank), 1) < rank

    def widen(index, _):
        for side in range(2):
            for base in range(0, half, piece):
                packed = user_full[index, base : base + piece, :].astype(jnp.float32)
                value = jnp.where(low, packed, 0.0) if side == 0 else jnp.where(low, 0.0, packed)
                place = index * 2 * half + side * half + base
                inside = pl.ds(pl.multiple_of(place % tile, piece), piece)
                user_wide[place // tile, inside, :] = value.astype(jnp.bfloat16)
        return 0

    lax.fori_loop(0, n_col, widen, 0)
    per_share = item_full.shape[1] // tile
    for index in range(n_row):
        for q in range(per_share):
            item_wide[index * per_share + q] = item_full[index, q * tile : (q + 1) * tile, :]

    def residual(s, _):
        for u in range(UNROLL):
            k = s * UNROLL + u
            left = user_wide[row_of[k]]
            right = item_wide[col_of[k]]
            product = lax.dot_general(
                left, right, (((1,), (1,)), ((), ())), preferred_element_type=jnp.float32
            )
            value = product - ratings[slot_of[k]].astype(jnp.float32)
            res[k] = value.astype(jnp.bfloat16)
        return 0

    lax.fori_loop(0, slots // UNROLL, residual, 0)

    def transposes(first, end):
        def some(s, _):
            for u in range(UNROLL):
                res_t[s * UNROLL + u] = res[from_slot[s * UNROLL + u]].T
            return 0

        lax.fori_loop(first, end, some, 0)

    def multiply(matrices, full, pick, way):
        for index in range(full.shape[0]):
            per = full.shape[1] // tile
            for q in range(per):
                basis_tiles[index * per + q] = full[index, q * tile : (q + 1) * tile, :]

        def some(s, _):
            total = sums_of[slots + 1]
            for u in range(2 * UNROLL):
                k = s * 2 * UNROLL + u
                part = jnp.dot(
                    matrices[k], basis_tiles[pick[k]], preferred_element_type=jnp.float32
                )
                total = part + keep[way * slots + k] * total
                sums_of[k] = total
            sums_of[slots + 1] = total
            return 0

        sums_of[slots + 1] = jnp.zeros(sums_of.shape[1:], jnp.float32)
        lax.fori_loop(0, slots // (2 * UNROLL), some, 0)

    start_gather.finish()

    panels = work.shape[0] // PANEL

    def eliminate_from(first):
        def panel(index, _):
            eliminate(work, index)
            return 0

        lax.fori_loop(first, panels, panel, 0)

    def apply(sums):
        return times_transposed(sums.own[0], inverse_factor(work))

    items_now = start_full
    for index in range(ITERS):
        last = index == ITERS - 1
        sums, gram, gather = forward_sums[index], grams[2 * index], user_gathers[index]
        multiply(res, items_now, col_of, 0)
        sums.send_products(lambda i: sums_of[user_last[i]])
        if index == 0:
            parts = slots // UNROLL // 3
            sums.pass_on(
                [functools.partial(transposes, parts * third, parts * (third + 1)) for third in range(3)]
            )
            sums.total()
        else:
            grams[2 * index - 1].collect(work)
            sums.pass_on([functools.partial(eliminate, work, panel) for panel in range(panels)])
            sums.total()
            sums.own[0] = apply(sums)
        gather.full[col.me] = sums.own[0].astype(jnp.bfloat16)
        gather.start()
        gram.begin(sums.own[0])
        gram.exchange()
        gather.forward(1)
        gram.spread()
        for t in range(2, col.outer):
            gather.forward(t)
        gram.collect(work)
        eliminate_from(0)
        if last:
            user_out[...] = apply(sums)
        gather.arrivals()
        sums, gram = backward_sums[index], grams[2 * index + 1]
        multiply(res_t, gather.full, back_row, 1)
        sums.send_products(lambda i: sums_of[item_last[i]])
        sums.pass_on()
        sums.total()
        sums.own[0] = apply(sums)
        if not last:
            gather = item_gathers[index]
            gather.full[row.me] = sums.own[0].astype(jnp.bfloat16)
            gather.start()
            gram.begin(sums.own[0])
            gather.finish()
            gram.exchange()
            gram.spread()
            items_now = gather.full
        else:
            gram.begin(sums.own[0])
            gram.exchange()
            gram.spread()
            gram.collect(work)
            eliminate_from(0)
            item_out[...] = apply(sums)

    for part in (
        [user_gather, item_gather, start_gather]
        + forward_sums
        + backward_sums
        + user_gathers
        + item_gathers
        + grams
    ):
        part.drain()


def shards(n_row, n_col, user_factors, item_factors, start_vectors, ratings, tile_rows, tile_cols, tile_count):
    slots, tile = ratings.shape[2], ratings.shape[-1]
    vecs = start_vectors.shape[1]
    users_share, rank = user_factors.shape
    items_share = item_factors.shape[0]
    users_block, items_block = users_share * n_col, items_share * n_row
    user_tiles, item_tiles = users_block // tile, items_block // tile
    number = jnp.arange(slots, dtype=jnp.int32)
    places = jnp.stack([tile_rows[0, 0], tile_cols[0, 0]])
    unused = user_tiles + item_tiles
    keys = jnp.where(number < tile_count[0, 0], places, unused)
    ranked = keys * slots + number
    rank_of = jnp.sum((ranked[:, None, :] < ranked[:, :, None]).astype(jnp.int32), axis=2)
    chosen = rank_of[:, None, :] == number[None, :, None]

    def pick(way, values):
        return jnp.sum(jnp.where(chosen[way], values[None, :], 0), axis=1)

    def last_of(way, tiles):
        target = jnp.arange(tiles, dtype=jnp.int32)[:, None]
        upto = jnp.sum((keys[way][None, :] <= target).astype(jnp.int32), axis=1)
        here = jnp.sum((keys[way][None, :] == target).astype(jnp.int32), axis=1)
        return jnp.where(here > 0, upto - 1, slots)

    def kept(way):
        earlier = (keys[way][None, :] == keys[way][:, None]) & (number[None, :] < number[:, None])
        return pick(way, jnp.any(earlier, axis=1).astype(jnp.int32)).astype(jnp.float32)

    tables = (
        pick(0, number),
        pick(0, places[0]),
        pick(0, places[1]),
        pick(1, rank_of[0]),
        pick(1, places[0]),
        jnp.concatenate([kept(0), kept(1)]),
        last_of(0, user_tiles),
        last_of(1, item_tiles),
    )
    half = users_share // 2
    users = jnp.concatenate([user_factors[:half], user_factors[half:]], axis=1)
    items = jnp.concatenate([item_factors, item_factors], axis=1)

    bf16, f32 = jnp.bfloat16, jnp.float32
    dma = pltpu.SemaphoreType.DMA

    def gather_sems(size):
        return [dma((size // 2,))] * 4

    def scatter_scratch(size, share):
        outer = size // 2
        return [
            pltpu.VMEM((outer, share, vecs), f32),
            pltpu.VMEM((outer, share, vecs), bf16),
            pltpu.VMEM((outer, share, vecs), bf16),
            pltpu.VMEM((outer, share, vecs), bf16),
            pltpu.VMEM((outer, share, vecs), bf16),
        ] + gather_sems(size)

    scratch = [
        pltpu.VMEM((n_col, half, 2 * rank), bf16),
        pltpu.VMEM((n_row, items_share, 2 * rank), bf16),
        pltpu.VMEM((n_row, items_share, vecs), bf16),
        pltpu.VMEM((user_tiles, tile, 2 * rank), bf16),
        pltpu.VMEM((item_tiles, tile, 2 * rank), bf16),
        pltpu.VMEM((slots, tile, tile), bf16),
        pltpu.VMEM((slots, tile, tile), bf16),
        pltpu.VMEM((max(user_tiles, item_tiles), tile, vecs), bf16),
        pltpu.VMEM((slots + 2, tile, vecs), f32),
        pltpu.VMEM((vecs, vecs), f32),
    ]
    scratch += gather_sems(n_col) + gather_sems(n_row) + gather_sems(n_row)
    for _ in range(ITERS):
        scratch += scatter_scratch(n_col, users_share)
        scratch += scatter_scratch(n_row, items_share)
        scratch += [pltpu.VMEM((n_col, users_share, vecs), bf16)] + gather_sems(n_col)
    for _ in range(ITERS - 1):
        scratch += [pltpu.VMEM((n_row, items_share, vecs), bf16)] + gather_sems(n_row)
    for _ in range(2 * ITERS):
        part = vecs // n_col
        scratch += [
            pltpu.VMEM((n_col, part, vecs), f32),
            pltpu.VMEM((n_col, part, vecs), f32),
            pltpu.VMEM((1, part, vecs), f32),
            pltpu.VMEM((n_row, part, vecs), f32),
            pltpu.VMEM((n_col, part, vecs), f32),
        ]
        scratch += [dma((n_col,)), dma((n_col,)), dma((n_row,)), dma((n_row,)), dma((n_col,)), dma((n_col,))]

    smem, vmem = pl.BlockSpec(memory_space=pltpu.SMEM), pl.BlockSpec(memory_space=pltpu.VMEM)
    user_basis, item_basis = pl.pallas_call(
        functools.partial(kernel, n_row, n_col),
        out_shape=(
            jax.ShapeDtypeStruct((users_share, vecs), f32),
            jax.ShapeDtypeStruct((items_share, vecs), f32),
        ),
        in_specs=[smem] * len(tables) + [vmem] * 4,
        out_specs=(vmem, vmem),
        scratch_shapes=scratch,
        compiler_params=pltpu.CompilerParams(
            collective_id=0, has_side_effects=True, vmem_limit_bytes=62 * 1024 * 1024
        ),
    )(*tables, users, items, start_vectors, ratings[0, 0])
    users_total = users_share * n_row * n_col
    items_total = items_share * n_row * n_col
    return (
        user_basis * jnp.sqrt(jnp.float32(users_total)),
        item_basis * jnp.sqrt(jnp.float32(items_total)),
    )


def solution(mesh):
    in_specs = (
        P(("row", "col"), None),
        P(("col", "row"), None),
        P(("col", "row"), None),
        P("row", "col", None, None, None),
        P("row", "col", None),
        P("row", "col", None),
        P("row", "col"),
    )
    out_specs = (P(("row", "col"), None), P(("col", "row"), None))
    body = functools.partial(shards, mesh.shape["row"], mesh.shape["col"])
    return jax.shard_map(body, mesh=mesh, in_specs=in_specs, out_specs=out_specs, check_vma=False)
```

```python
import functools
import math

import jax
import jax.numpy as jnp
from jax import lax
from jax.experimental import pallas as pl
from jax.experimental.pallas import tpu as pltpu
from jax.sharding import PartitionSpec as P

MESH = pl.DeviceIdType.MESH
HIGHEST = lax.Precision.HIGHEST
ITERS = 2
UNROLL = 8
TILE = 128
PANEL = 32
SUB = 8


def aligned(index, size):
    return pl.ds(pl.multiple_of(index * size, size), size)


class Group:
    def __init__(self, axis, size, other_axis):
        self.axis = axis
        self.size = size
        self.outer = size // 2
        self.me = lax.axis_index(axis)
        self.other = lax.axis_index(other_axis)
        self.o = self.me // 2
        self.i = self.me % 2

    def device(self, index):
        if self.axis == "col":
            return (self.other, index)
        return (index, self.other)

    def ahead(self, t):
        return (self.o + t) % self.outer

    def behind(self, t):
        return (self.o + self.outer - t) % self.outer


def remote(src, dst, send, recv, device):
    return pltpu.make_async_remote_copy(
        src_ref=src, dst_ref=dst, send_sem=send, recv_sem=recv, device_id=device, device_id_type=MESH
    )


class Gather:
    def __init__(self, group, full, sems):
        self.group, self.full = group, full
        self.outer_send, self.outer_recv, self.inner_send, self.inner_recv = sems

    def outer_copy(self, t):
        g = self.group
        block = self.full.at[g.me]
        return remote(
            block, block, self.outer_send.at[t], self.outer_recv.at[t], g.device(g.ahead(t) * 2 + g.i)
        )

    def outer_arrival(self, t):
        g = self.group
        block = self.full.at[g.behind(t) * 2 + g.i]
        return remote(
            block, block, self.outer_send.at[t], self.outer_recv.at[t], g.device(g.ahead(t) * 2 + g.i)
        )

    def inner_copy(self, t):
        g = self.group
        block = self.full.at[g.behind(t) * 2 + g.i]
        return remote(
            block, block, self.inner_send.at[t], self.inner_recv.at[t], g.device(g.o * 2 + 1 - g.i)
        )

    def inner_arrival(self, t):
        g = self.group
        block = self.full.at[g.behind(t) * 2 + 1 - g.i]
        return remote(
            block, block, self.inner_send.at[t], self.inner_recv.at[t], g.device(g.o * 2 + 1 - g.i)
        )

    def start(self):
        for t in range(self.group.outer - 1, 0, -1):
            self.outer_copy(t).start()
        self.inner_copy(0).start()

    def forward(self, t):
        self.outer_arrival(t).wait_recv()
        self.inner_copy(t).start()

    def finish(self):
        for t in range(1, self.group.outer):
            self.forward(t)
        self.arrivals()

    def arrivals(self):
        for t in range(self.group.outer):
            self.inner_arrival(t).wait_recv()

    def drain(self):
        for t in range(1, self.group.outer):
            self.outer_copy(t).wait_send()
        for t in range(self.group.outer):
            self.inner_copy(t).wait_send()


class Scatter:
    def __init__(self, group, own, inner_out, inner_in, outer_out, outer_in, sems):
        self.group = group
        self.own, self.inner_out, self.inner_in = own, inner_out, inner_in
        self.outer_out, self.outer_in = outer_out, outer_in
        self.outer_send, self.outer_recv, self.inner_send, self.inner_recv = sems

    def inner_copy(self, t):
        g = self.group
        return remote(
            self.inner_out.at[t],
            self.inner_in.at[t],
            self.inner_send.at[t],
            self.inner_recv.at[t],
            g.device(g.o * 2 + 1 - g.i),
        )

    def outer_copy(self, t):
        g = self.group
        return remote(
            self.outer_out.at[t],
            self.outer_in.at[t],
            self.outer_send.at[t],
            self.outer_recv.at[t],
            g.device(g.ahead(t) * 2 + g.i),
        )

    def send_products(self, fetch):
        g = self.group
        share = self.own.shape[1]
        per = share // TILE

        def step(s, _):
            t = (s + 1) % g.outer
            there = g.ahead(t)
            for q in range(per):
                place = pl.ds(q * TILE, TILE)
                tile = fetch((there * 2 + 1 - g.i) * per + q)
                self.inner_out[t, place, :] = tile.astype(jnp.bfloat16)
            self.inner_copy(t).start()
            for q in range(per):
                self.own[t, pl.ds(q * TILE, TILE), :] = fetch((there * 2 + g.i) * per + q)
            return 0

        lax.fori_loop(0, g.outer, step, 0)

    def pass_on(self, beside=()):
        beside = list(beside)

        def step(t):
            self.inner_copy(t).wait_recv()
            self.outer_out[t] = (self.own[t] + self.inner_in[t].astype(jnp.float32)).astype(
                jnp.bfloat16
            )
            self.outer_copy(t).start()

        for t in range(1, self.group.outer):
            step(t)
            if beside:
                beside.pop(0)()
        for part in beside:
            part()

    def total(self):
        self.inner_copy(0).wait_recv()
        self.own[0] = self.own[0] + self.inner_in[0].astype(jnp.float32)

        def step(t, _):
            self.outer_copy(t).wait_recv()
            self.own[0] = self.own[0] + self.outer_in[t].astype(jnp.float32)
            return 0

        lax.fori_loop(1, self.group.outer, step, 0)

    def drain(self):
        for t in range(1, self.group.outer):
            self.outer_copy(t).wait_send()
        for t in range(self.group.outer):
            self.inner_copy(t).wait_send()


class Gram:
    def __init__(self, row, col, parts, arrived, mine, others, full, sems):
        self.row, self.col = row, col
        self.parts, self.arrived, self.mine, self.others, self.full = parts, arrived, mine, others, full
        self.sems = sems

    def scatter_copy(self, t):
        c = self.col
        there = (c.me + t) % c.size
        return remote(
            self.parts.at[there],
            self.arrived.at[t],
            self.sems[0].at[t],
            self.sems[1].at[t],
            c.device(there),
        )

    def exchange_copy(self, t):
        r = self.row
        return remote(
            self.mine.at[0],
            self.others.at[t],
            self.sems[2].at[t],
            self.sems[3].at[t],
            r.device((r.me + t) % r.size),
        )

    def gather_copy(self, t):
        c = self.col
        return remote(
            self.full.at[c.me],
            self.full.at[c.me],
            self.sems[4].at[t],
            self.sems[5].at[t],
            c.device((c.me + t) % c.size),
        )

    def gather_arrival(self, t):
        c = self.col
        block = self.full.at[(c.me + c.size - t) % c.size]
        return remote(
            block, block, self.sems[4].at[t], self.sems[5].at[t], c.device((c.me + t) % c.size)
        )

    def begin(self, block):
        gram = lax.dot_general(
            block, block, (((0,), (0,)), ((), ())), precision=HIGHEST, preferred_element_type=jnp.float32
        )
        rows = self.parts.shape[1]
        for index in range(self.col.size):
            self.parts[index] = gram[index * rows : (index + 1) * rows, :]
        for t in range(1, self.col.size):
            self.scatter_copy(t).start()

    def exchange(self):
        for t in range(1, self.col.size):
            self.scatter_copy(t).wait_recv()
        total = self.parts[self.col.me]
        for t in range(1, self.col.size):
            total = total + self.arrived[t]
        self.mine[0] = total
        for t in range(1, self.row.size):
            self.exchange_copy(t).start()

    def spread(self):
        for t in range(1, self.row.size):
            self.exchange_copy(t).wait_recv()
        total = self.mine[0]
        for t in range(1, self.row.size):
            total = total + self.others[t]
        self.full[self.col.me] = total
        for t in range(1, self.col.size):
            self.gather_copy(t).start()

    def collect(self, work):
        for t in range(1, self.col.size):
            self.gather_arrival(t).wait_recv()
        rows = self.parts.shape[1]
        for index in range(self.col.size):
            work[index * rows : (index + 1) * rows, :] = self.full[index]

    def drain(self):
        for t in range(1, self.col.size):
            self.scatter_copy(t).wait_send()
            self.gather_copy(t).wait_send()
        for t in range(1, self.row.size):
            self.exchange_copy(t).wait_send()


def eliminate(work, panel):
    size = work.shape[0]
    base = panel * PANEL if isinstance(panel, int) else pl.multiple_of(panel * PANEL, PANEL)
    lanes = lax.broadcasted_iota(jnp.int32, (PANEL, size), 1)
    subs = lax.broadcasted_iota(jnp.int32, (PANEL, size), 0)
    done, active = [], work[pl.ds(base, PANEL), :]
    for q in range(PANEL // SUB):
        lane, sub = lanes[q * SUB :], subs[: PANEL - q * SUB]
        columns = []
        for b in range(SUB):
            picked = jnp.where(lane == base + q * SUB + b, active, 0.0)
            columns.append(jnp.broadcast_to(jnp.sum(picked, axis=1, keepdims=True), active.shape))
        for a in range(SUB):
            here = lane == base + q * SUB + a
            inverse = 1.0 / columns[a][a : a + 1, :]
            factor = jnp.where(sub > a, columns[a] * inverse, 0.0)
            row = jnp.where(here[:1], 1.0, active[a : a + 1, :])
            active = jnp.where(here & (sub > a), 0.0, active) - factor * row
            for b in range(a + 1, SUB):
                columns[b] = columns[b] - factor * columns[b][a : a + 1, :]
        done.append(active[:SUB])
        active = active[SUB:]
    rows = jnp.concatenate(done, axis=0)
    work[pl.ds(base, PANEL), :] = rows
    diagonal = lanes == base + subs
    pivots = jnp.sum(jnp.where(diagonal, rows, 0.0), axis=1, keepdims=True)
    inside = (lanes >= base) & (lanes < base + PANEL)
    factors = jnp.where(lanes >= base + PANEL, rows, 0.0) / pivots
    full = jnp.where(inside & (lanes > base + subs), 0.0, jnp.where(diagonal, 1.0, rows))
    update = lax.dot_general(
        factors, full, (((0,), (0,)), ((), ())), precision=HIGHEST, preferred_element_type=jnp.float32
    )
    lane = lax.broadcasted_iota(jnp.int32, (size, size), 1)
    sub = lax.broadcasted_iota(jnp.int32, (size, size), 0)
    fresh = (lane >= base) & (lane < base + PANEL) & (sub >= base + PANEL)
    work[...] = jnp.where(fresh, 0.0, work[...]) - update


def inverse_factor(work):
    size = work.shape[0]
    lanes = lax.broadcasted_iota(jnp.int32, (size, size), 1)
    subs = lax.broadcasted_iota(jnp.int32, (size, size), 0)
    matrix = work[...]
    pivots = jnp.sum(jnp.where(lanes == subs, matrix, 0.0), axis=1, keepdims=True)
    unit = jnp.where(lanes == subs, 1.0, jnp.where(lanes < subs, matrix, 0.0))
    return unit * lax.rsqrt(pivots)


def times_transposed(block, inverse):
    return lax.dot_general(
        block, inverse, (((1,), (1,)), ((), ())), precision=HIGHEST, preferred_element_type=jnp.float32
    )


def kernel(n_row, n_col, *refs):
    refs = list(refs)

    def take(count):
        got = refs[:count]
        del refs[:count]
        return got

    slot_of, row_of, col_of, from_slot, back_row, user_keep, item_keep, user_last, item_last = take(9)
    users, items, start, ratings_far = take(4)
    user_out, item_out = take(2)
    user_full, item_full, start_full, user_wide, item_wide, res, res_t, basis_tiles, sums_of, work, ratings, rating_sem = take(12)
    row = Group("row", n_row, "col")
    col = Group("col", n_col, "row")
    user_gather = Gather(col, user_full, take(4))
    item_gather = Gather(row, item_full, take(4))
    start_gather = Gather(row, start_full, take(4))
    forward_sums, backward_sums, user_gathers, item_gathers, grams = [], [], [], [], []
    for _ in range(ITERS):
        forward_sums.append(Scatter(col, *take(5), take(4)))
        backward_sums.append(Scatter(row, *take(5), take(4)))
        user_gathers.append(Gather(col, *take(1), take(4)))
    for _ in range(ITERS - 1):
        item_gathers.append(Gather(row, *take(1), take(4)))
    for _ in range(2 * ITERS):
        grams.append(Gram(col, row, *take(5), take(6)))
    assert not refs

    loading = pltpu.make_async_copy(ratings_far, ratings, rating_sem)
    loading.start()
    barrier = pltpu.get_barrier_semaphore()
    for group in (row, col):
        for t in range(1, group.size):
            pl.semaphore_signal(
                barrier, inc=1, device_id=group.device((group.me + t) % group.size), device_id_type=MESH
            )
    pl.semaphore_wait(barrier, n_row + n_col - 2)

    half, rank = users.shape[0] // 2, users.shape[1]
    user_full[col.me] = jnp.concatenate([users[:half, :], users[half:, :]], axis=1)
    user_gather.start()
    item_full[row.me] = jnp.concatenate([items[...], items[...]], axis=1)
    item_gather.start()
    start_full[row.me] = start[...]
    start_gather.start()

    slots, tile, _ = ratings.shape
    sums_of[slots] = jnp.zeros(sums_of.shape[1:], jnp.float32)

    item_gather.finish()
    user_gather.finish()

    piece = min(half, tile)
    low = lax.broadcasted_iota(jnp.int32, (piece, 2 * rank), 1) < rank

    def widen(index, _):
        for side in range(2):
            for base in range(0, half, piece):
                packed = user_full[index, base : base + piece, :].astype(jnp.float32)
                value = jnp.where(low, packed, 0.0) if side == 0 else jnp.where(low, 0.0, packed)
                place = index * 2 * half + side * half + base
                inside = pl.ds(pl.multiple_of(place % tile, piece), piece)
                user_wide[place // tile, inside, :] = value.astype(jnp.bfloat16)
        return 0

    lax.fori_loop(0, n_col, widen, 0)
    per_share = item_full.shape[1] // tile
    for index in range(n_row):
        for q in range(per_share):
            item_wide[index * per_share + q] = item_full[index, q * tile : (q + 1) * tile, :]

    loading.wait()

    def residual(s, _):
        for u in range(UNROLL):
            k = s * UNROLL + u
            left = user_wide[row_of[k]]
            right = item_wide[col_of[k]]
            product = lax.dot_general(
                left, right, (((1,), (1,)), ((), ())), preferred_element_type=jnp.float32
            )
            value = product - ratings[slot_of[k]].astype(jnp.float32)
            res[k] = value.astype(jnp.bfloat16)
        return 0

    lax.fori_loop(0, slots // UNROLL, residual, 0)

    def transposes(first, end):
        def some(s, _):
            for u in range(UNROLL):
                res_t[s * UNROLL + u] = res[from_slot[s * UNROLL + u]].T
            return 0

        lax.fori_loop(first, end, some, 0)

    def multiply(matrices, full, pick, keep):
        for index in range(full.shape[0]):
            per = full.shape[1] // tile
            for q in range(per):
                basis_tiles[index * per + q] = full[index, q * tile : (q + 1) * tile, :]

        def some(s, _):
            total = sums_of[slots + 1]
            for u in range(UNROLL):
                k = s * UNROLL + u
                part = jnp.dot(
                    matrices[k], basis_tiles[pick[k]], preferred_element_type=jnp.float32
                )
                total = part + keep[k] * total
                sums_of[k] = total
            sums_of[slots + 1] = total
            return 0

        sums_of[slots + 1] = jnp.zeros(sums_of.shape[1:], jnp.float32)
        lax.fori_loop(0, slots // (UNROLL), some, 0)

    start_gather.finish()

    panels = work.shape[0] // PANEL

    def eliminate_from(first):
        def panel(index, _):
            eliminate(work, index)
            return 0

        lax.fori_loop(first, panels, panel, 0)

    def apply(sums):
        return times_transposed(sums.own[0], inverse_factor(work))

    items_now = start_full
    for index in range(ITERS):
        last = index == ITERS - 1
        sums, gram, gather = forward_sums[index], grams[2 * index], user_gathers[index]
        multiply(res, items_now, col_of, user_keep)
        sums.send_products(lambda i: sums_of[user_last[i]])
        if index == 0:
            parts = slots // UNROLL // 3
            sums.pass_on(
                [functools.partial(transposes, parts * third, parts * (third + 1)) for third in range(3)]
            )
            sums.total()
        else:
            grams[2 * index - 1].collect(work)
            sums.pass_on([functools.partial(eliminate, work, panel) for panel in range(panels)])
            sums.total()
            sums.own[0] = apply(sums)
        gather.full[col.me] = sums.own[0].astype(jnp.bfloat16)
        gather.start()
        gram.begin(sums.own[0])
        gram.exchange()
        gather.forward(1)
        gram.spread()
        for t in range(2, col.outer):
            gather.forward(t)
        gram.collect(work)
        eliminate_from(0)
        if last:
            user_out[...] = apply(sums) * math.sqrt(user_out.shape[0] * n_row * n_col)
        gather.arrivals()
        sums, gram = backward_sums[index], grams[2 * index + 1]
        multiply(res_t, gather.full, back_row, item_keep)
        sums.send_products(lambda i: sums_of[item_last[i]])
        sums.pass_on()
        sums.total()
        sums.own[0] = apply(sums)
        if not last:
            gather = item_gathers[index]
            gather.full[row.me] = sums.own[0].astype(jnp.bfloat16)
            gather.start()
            gram.begin(sums.own[0])
            gather.finish()
            gram.exchange()
            gram.spread()
            items_now = gather.full
        else:
            gram.begin(sums.own[0])
            gram.exchange()
            gram.spread()
            gram.collect(work)
            eliminate_from(0)
            item_out[...] = apply(sums) * math.sqrt(item_out.shape[0] * n_row * n_col)

    for part in (
        [user_gather, item_gather, start_gather]
        + forward_sums
        + backward_sums
        + user_gathers
        + item_gathers
        + grams
    ):
        part.drain()


def shards(n_row, n_col, user_factors, item_factors, start_vectors, ratings, tile_rows, tile_cols, tile_count):
    slots, tile = ratings.shape[2], ratings.shape[-1]
    vecs = start_vectors.shape[1]
    users_share, rank = user_factors.shape
    items_share = item_factors.shape[0]
    users_block, items_block = users_share * n_col, items_share * n_row
    user_tiles, item_tiles = users_block // tile, items_block // tile
    number = jnp.arange(slots, dtype=jnp.int32)
    places = jnp.stack([tile_rows[0, 0], tile_cols[0, 0]])
    unused = user_tiles + item_tiles
    keys = jnp.where(number < tile_count[0, 0], places, unused)
    ranked = keys * slots + number
    rank_of = jnp.sum((ranked[:, None, :] < ranked[:, :, None]).astype(jnp.int32), axis=2)
    chosen = rank_of[:, None, :] == number[None, :, None]

    def pick(way, values):
        return jnp.sum(jnp.where(chosen[way], values[None, :], 0), axis=1)

    def last_of(way, tiles):
        target = jnp.arange(tiles, dtype=jnp.int32)[:, None]
        upto = jnp.sum((keys[way][None, :] <= target).astype(jnp.int32), axis=1)
        here = jnp.sum((keys[way][None, :] == target).astype(jnp.int32), axis=1)
        return jnp.where(here > 0, upto - 1, slots)

    def kept(way):
        earlier = (keys[way][None, :] == keys[way][:, None]) & (number[None, :] < number[:, None])
        return pick(way, jnp.any(earlier, axis=1).astype(jnp.int32)).astype(jnp.float32)

    tables = (
        pick(0, number),
        pick(0, places[0]),
        pick(0, places[1]),
        pick(1, rank_of[0]),
        pick(1, places[0]),
        kept(0),
        kept(1),
        last_of(0, user_tiles),
        last_of(1, item_tiles),
    )
    half = users_share // 2

    bf16, f32 = jnp.bfloat16, jnp.float32
    dma = pltpu.SemaphoreType.DMA

    def gather_sems(size):
        return [dma((size // 2,))] * 4

    def scatter_scratch(size, share):
        outer = size // 2
        return [
            pltpu.VMEM((outer, share, vecs), f32),
            pltpu.VMEM((outer, share, vecs), bf16),
            pltpu.VMEM((outer, share, vecs), bf16),
            pltpu.VMEM((outer, share, vecs), bf16),
            pltpu.VMEM((outer, share, vecs), bf16),
        ] + gather_sems(size)

    scratch = [
        pltpu.VMEM((n_col, half, 2 * rank), bf16),
        pltpu.VMEM((n_row, items_share, 2 * rank), bf16),
        pltpu.VMEM((n_row, items_share, vecs), bf16),
        pltpu.VMEM((user_tiles, tile, 2 * rank), bf16),
        pltpu.VMEM((item_tiles, tile, 2 * rank), bf16),
        pltpu.VMEM((slots, tile, tile), bf16),
        pltpu.VMEM((slots, tile, tile), bf16),
        pltpu.VMEM((max(user_tiles, item_tiles), tile, vecs), bf16),
        pltpu.VMEM((slots + 2, tile, vecs), f32),
        pltpu.VMEM((vecs, vecs), f32),
        pltpu.VMEM((slots, tile, tile), bf16),
        dma,
    ]
    scratch += gather_sems(n_col) + gather_sems(n_row) + gather_sems(n_row)
    for _ in range(ITERS):
        scratch += scatter_scratch(n_col, users_share)
        scratch += scatter_scratch(n_row, items_share)
        scratch += [pltpu.VMEM((n_col, users_share, vecs), bf16)] + gather_sems(n_col)
    for _ in range(ITERS - 1):
        scratch += [pltpu.VMEM((n_row, items_share, vecs), bf16)] + gather_sems(n_row)
    for _ in range(2 * ITERS):
        part = vecs // n_row
        scratch += [
            pltpu.VMEM((n_row, part, vecs), f32),
            pltpu.VMEM((n_row, part, vecs), f32),
            pltpu.VMEM((1, part, vecs), f32),
            pltpu.VMEM((n_col, part, vecs), f32),
            pltpu.VMEM((n_row, part, vecs), f32),
        ]
        scratch += [dma((n_row,)), dma((n_row,)), dma((n_col,)), dma((n_col,)), dma((n_row,)), dma((n_row,))]

    smem, vmem = pl.BlockSpec(memory_space=pltpu.SMEM), pl.BlockSpec(memory_space=pltpu.VMEM)
    user_basis, item_basis = pl.pallas_call(
        functools.partial(kernel, n_row, n_col),
        out_shape=(
            jax.ShapeDtypeStruct((users_share, vecs), f32),
            jax.ShapeDtypeStruct((items_share, vecs), f32),
        ),
        in_specs=[smem] * len(tables) + [vmem] * 3 + [pl.BlockSpec(memory_space=pl.ANY)],
        out_specs=(vmem, vmem),
        scratch_shapes=scratch,
        compiler_params=pltpu.CompilerParams(
            collective_id=0, has_side_effects=True, vmem_limit_bytes=62 * 1024 * 1024
        ),
    )(*tables, user_factors, item_factors, start_vectors, ratings[0, 0])
    return user_basis, item_basis


def solution(mesh):
    in_specs = (
        P(("row", "col"), None),
        P(("col", "row"), None),
        P(("col", "row"), None),
        P("row", "col", None, None, None),
        P("row", "col", None),
        P("row", "col", None),
        P("row", "col"),
    )
    out_specs = (P(("row", "col"), None), P(("col", "row"), None))
    body = functools.partial(shards, mesh.shape["row"], mesh.shape["col"])
    return jax.shard_map(body, mesh=mesh, in_specs=in_specs, out_specs=out_specs, check_vma=False)
```
